128 devices in a mesh: dom: 4 (over x), col: 32 (over z, y, core).
Axes of the slice: x: 4, y: 4, z: 4, core: 2. Of those that a mesh axis runs over, the one named last changes fastest.
Arguments:
- ensemble: float32 [128, 5, 96, 4096], P('dom', None, None, 'col'), may hold values from -6 to 6
- depth_class: int32 [96, 4096], P(None, 'col'), may hold values from 0 to 7
- obs_index: int32 [24576], P('col'), may hold values from 0 to 12287
- obs_value: float32 [24576], P('col'), may hold values from -4 to 16
- annealing_exponents: float32 [96, 4096], P(None, 'col'), may hold values from 0.05 to 1
Outputs:
- posterior: float32 [5, 96, 4096], P(None, None, 'col')
The draws below stay inside these ranges and needn't reach their ends.
Inputs may be any that keep to these rules, and one draw needn't show every extreme that they name: `obs_index`: each entry is a cell of its own block of 128 columns, numbered row * 128 + column within the block; entries may repeat.
All inputs are finite; a program needn't handle non-finite values.
Results may differ from the reference program's by a relative error of at most 0.0003.
Values sent between devices are 32-bit elements; how exact they have to be, the bound alone decides.
A program may use at most 128 MiB of HBM per device.

```python
import math
import jax
import jax.numpy as jnp
from jax import lax

FIELDS = 5
ROWS = 96
COL_DEV = 128
ROW_REACH = 8
RADIUS = 64
OBS_DEV = 768
MEMBERS = 128
COLS = 4096
NOBS = 24576
N_COL = 32


def draw_annealing_exponents(key, part):
    unit = jax.random.uniform(key, (ROWS, COLS), jnp.float32)
    return jnp.exp(math.log(0.05) + unit * math.log(20.0))


def draw_obs_value(key, part):
    blocks = NOBS // OBS_DEV
    key_noise = jax.random.fold_in(key, 11)
    key_bits = jax.random.fold_in(key, 12)
    key_pick = jax.random.fold_in(key, 13)
    bits_drawn = jax.random.randint(key_bits, (blocks,), 0, 2)
    forced = jax.random.randint(key_pick, (), 0, blocks)
    chosen = jnp.maximum(bits_drawn, (jnp.arange(blocks) == forced).astype(jnp.int32))
    offset = 12.0 * chosen.astype(jnp.float32)
    noise = jnp.clip(jax.random.normal(key_noise, (blocks, OBS_DEV), jnp.float32), -4.0, 4.0)
    return (noise + offset[:, None]).reshape(NOBS)


def set_ends(result, key, least, high):
    spot = [jax.random.randint(jax.random.fold_in(key, axis), (), 0, length) for axis, length in enumerate(result.shape)]
    widest = result.shape.index(max(result.shape))
    beside = spot[:widest] + [(spot[widest] + 1) % result.shape[widest]] + spot[widest + 1:]
    return result.at[tuple(spot)].set(least).at[tuple(beside)].set(high)


def shard_levels(key, dims, pieces, low, largest):
    def one(dim, parts):
        steps = jax.random.uniform(jax.random.fold_in(jax.random.fold_in(key, 6), dim), (parts,), jnp.float32, low / len(pieces), largest / len(pieces))
        return jnp.repeat(jnp.exp(steps), dims[dim] // parts).reshape((-1,) + (1,) * (len(dims) - dim - 1))

    level = one(*pieces[0])
    for cut in pieces[1:]:
        level = level * one(*cut)
    return level


def bell_draw(own_key, dims, width, most, pieces=(), kind=jnp.bfloat16):
    values = jax.random.normal(own_key, dims, jnp.float32) * width
    if len(pieces) > 0:
        values = shard_levels(own_key, dims, pieces, -0.22, 0.18) * values
    return jnp.clip(values, min=-most, max=most).astype(kind)


def setup_inputs(seed: int = 0) -> dict:
    arg_keys = jax.random.split(jax.random.key(seed), 6)
    ensemble = bell_draw(arg_keys[0], (MEMBERS, FIELDS, ROWS, COLS), 1.0, 6.0, ((0, 4), (3, 32)), jnp.float32)
    depth_class = set_ends(jax.random.randint(arg_keys[1], (ROWS, COLS), 0, 8), jax.random.fold_in(arg_keys[1], 1), 0, 7).astype(jnp.int32)
    obs_index = set_ends(jax.random.randint(arg_keys[2], (NOBS,), 0, ROWS * COL_DEV), jax.random.fold_in(arg_keys[2], 1), 0, (ROWS * COL_DEV) - 1).astype(jnp.int32)
    obs_value = draw_obs_value(jax.random.fold_in(arg_keys[5], 71), 0)
    annealing_exponents = draw_annealing_exponents(jax.random.fold_in(arg_keys[5], 71), 0)
    return {"ensemble": ensemble, "depth_class": depth_class, "obs_index": obs_index, "obs_value": obs_value, "annealing_exponents": annealing_exponents}


TIME_STEP = 0.25
CORIOLIS = 0.2


def diff_cols(field):
    return 0.5 * (field[..., 2:] - field[..., :-2])


def diff_rows(field):
    padded = jnp.pad(field, [(0, 0)] * (field.ndim - 2) + [(1, 1), (0, 0)])
    return 0.5 * (padded[..., 2:, :] - padded[..., :-2, :])


def integrate_model_ahead(solution_vector, bathymetry_points):
    height = solution_vector[..., 0, :, :]
    zonal_flow = solution_vector[..., 1, :, :]
    meridional = solution_vector[..., 2, :, :]
    tracers = solution_vector[..., 3:, :, :]
    zonal_new = zonal_flow[..., 1:-1] - TIME_STEP * diff_cols(height) + TIME_STEP * CORIOLIS * meridional[..., 1:-1]
    merid_new = meridional[..., 1:-1] - TIME_STEP * diff_rows(height)[..., 1:-1] - TIME_STEP * CORIOLIS * zonal_flow[..., 1:-1]
    inner_depth = bathymetry_points[..., 1:-1]
    height_new = height[..., 2:-2] - TIME_STEP * (diff_cols(inner_depth * zonal_new) + diff_rows(inner_depth * merid_new)[..., 1:-1])
    tracer_new = tracers[..., 2:-2] - TIME_STEP * (zonal_new[..., None, :, 1:-1] * diff_cols(tracers)[..., 1:-1] + merid_new[..., None, :, 1:-1] * diff_rows(tracers)[..., 2:-2])
    return jnp.concatenate([height_new[..., None, :, :], zonal_new[..., None, :, 1:-1], merid_new[..., None, :, 1:-1], tracer_new], axis=-3)


def smoothing_tables(number_of_meridional_lines, reach, number_of_lateral_lines, radius):
    row_ids = jnp.arange(number_of_meridional_lines).astype(jnp.float32)
    rows_table = jnp.maximum(0.0, 1.0 - jnp.abs(row_ids[:, None] - row_ids[None, :]) / (reach + 1.0))
    span_ids = jnp.arange(number_of_lateral_lines + 2 * radius).astype(jnp.float32)
    target_ids = jnp.arange(number_of_lateral_lines).astype(jnp.float32)
    cols_table = jnp.maximum(0.0, 1.0 - jnp.abs(span_ids[:, None] - radius - target_ids[None, :]) / (radius + 1.0))
    return rows_table, cols_table


def periodic_lateral_lines(field, extra):
    return jnp.concatenate([field[..., -extra:], field, field[..., :extra]], axis=-1)


def reference(ensemble, depth_class, obs_index, obs_value, annealing_exponents):
    bathymetry_points = 0.5 + 0.25 * depth_class.astype(jnp.float32)
    bathymetry_broadened = periodic_lateral_lines(bathymetry_points, 2)
    owner_block = jnp.arange(NOBS, dtype=jnp.int32) // OBS_DEV
    domainwide_point_number = (obs_index // COL_DEV) * COLS + owner_block * COL_DEV + obs_index % COL_DEV
    rows_table, cols_table = smoothing_tables(ROWS, ROW_REACH, COL_DEV, RADIUS)

    def ensemble_mismatch_parts(ensemble_slot):
        halfway_solution = integrate_model_ahead(periodic_lateral_lines(ensemble_slot, 2), bathymetry_broadened)
        prior_solution = integrate_model_ahead(periodic_lateral_lines(halfway_solution, 2), bathymetry_broadened)
        prognosed_solution = prior_solution[0].reshape(-1)[domainwide_point_number]
        misfit = obs_value - prognosed_solution
        loglik = jnp.zeros((ROWS * COLS,), jnp.float32).at[domainwide_point_number].add(-0.5 * misfit * misfit).reshape(ROWS, COLS)
        smoothed = jnp.dot(rows_table, loglik, precision=lax.Precision.HIGHEST)
        widened = periodic_lateral_lines(smoothed, RADIUS)
        windows = jnp.stack([widened[:, block_index * COL_DEV: block_index * COL_DEV + COL_DEV + 2 * RADIUS] for block_index in range(N_COL)])
        filtered_lateral_lines = jnp.einsum("brk,kc->rbc", windows, cols_table, precision=lax.Precision.HIGHEST).reshape(ROWS, COLS)
        return prior_solution, annealing_exponents * filtered_lateral_lines

    def absorb(running, ensemble_slot):
        peak_value, importance_aggregate, importance_scaled_solution = running
        prior_solution, logarithmic_importance = ensemble_mismatch_parts(ensemble_slot)
        revised_maximum = jnp.maximum(peak_value, logarithmic_importance)
        normalize_importance = jnp.exp(peak_value - revised_maximum)
        sample_importance = jnp.exp(logarithmic_importance - revised_maximum)
        return (revised_maximum, importance_aggregate * normalize_importance + sample_importance, importance_scaled_solution * normalize_importance[None] + sample_importance[None] * prior_solution), None

    start = (jnp.full((ROWS, COLS), -1.0e30, jnp.float32), jnp.zeros((ROWS, COLS), jnp.float32), jnp.zeros((FIELDS, ROWS, COLS), jnp.float32))
    final, unused = lax.scan(absorb, start, ensemble)
    return final[2] / final[1][None]
```

```python
import functools

import jax
import jax.numpy as jnp
from jax import lax
from jax.experimental import pallas as pl
from jax.experimental.pallas import tpu as pltpu
from jax.sharding import PartitionSpec as P

MESH = pl.DeviceIdType.MESH
F32 = jnp.float32
BF16 = jnp.bfloat16

TIME_STEP = 0.25
CORIOLIS = 0.2
HALF_DT = 0.5 * TIME_STEP
DT_F = TIME_STEP * CORIOLIS

ROW_REACH = 8
LANES = 128
PAD = 8
FOLD = 8
SPAN = 16
CHUNK = 32


def east(q):
    return pltpu.roll(q, LANES - 1, q.ndim - 1)


def west(q):
    return pltpu.roll(q, 1, q.ndim - 1)


def shifted(q, amount):
    return pltpu.roll(q, amount % LANES, q.ndim - 1)


def pieces(q):
    first = q.astype(BF16)
    rest = q - first.astype(F32)
    second = rest.astype(BF16)
    third = (rest - second.astype(F32)).astype(BF16)
    return first, second, third


def lane_of(shape):
    return lax.broadcasted_iota(jnp.int32, shape, len(shape) - 1)


def row_of(shape):
    return lax.broadcasted_iota(jnp.int32, shape, len(shape) - 2)


def dot(a, b):
    return jnp.dot(a, b, preferred_element_type=F32)


def kernel(
    n_dom,
    n_col,
    ens_ref,
    class_ref,
    where_ref,
    value_ref,
    anneal_ref,
    out_ref,
    X,
    Y,
    DV,
    HP,
    D,
    Q,
    FE,
    SL,
    SR,
    RL,
    RR,
    OBS,
    SM,
    PART,
    TOL,
    TOR,
    HL,
    HR,
    LW,
    GIVE,
    TAKE,
    RT,
    WOWN,
    WHALO,
    load_sem,
    edge_send,
    edge_recv,
    depth_send,
    depth_recv,
    halo_send,
    halo_recv,
    part_send,
    part_recv,
    out_send,
    out_recv,
):
    members, fields, rows, _ = ens_ref.shape
    groups = members // FOLD
    pairs = members // 2
    share = rows // n_dom
    radius = LANES // 2
    me_dom = lax.axis_index("dom")
    me_col = lax.axis_index("col")
    right = lax.rem(me_col + 1, n_col)
    left = lax.rem(me_col + n_col - 1, n_col)

    def load(g):
        return pltpu.make_async_copy(
            ens_ref.at[pl.ds(g * FOLD, FOLD)],
            X.at[pl.ds(g * FOLD, FOLD), :, pl.ds(PAD, rows), :],
            load_sem.at[g],
        )

    for g in range(groups):
        load(g).start()

    barrier = pltpu.get_barrier_semaphore()
    for other in (left, right):
        pl.semaphore_signal(barrier, inc=1, device_id=(me_dom, other), device_id_type=MESH)
    for off in range(1, n_dom):
        pl.semaphore_signal(
            barrier,
            inc=1,
            device_id=(lax.rem(me_dom + off, n_dom), me_col),
            device_id_type=MESH,
        )

    zero = jnp.zeros((PAD, LANES), F32)

    def clear(m, carry):
        for f in (0, 3, 4):
            X[m, f, 0:PAD, :] = zero
            X[m, f, PAD + rows : PAD + rows + PAD, :] = zero
        return carry

    lax.fori_loop(0, members + 2 * groups, clear, 0)
    for f in (0, 3, 4):
        Y[f, 0:PAD, :] = zero
        Y[f, PAD + rows : PAD + rows + PAD, :] = zero
    DV[0:PAD, :] = zero
    DV[PAD + rows : PAD + rows + PAD, :] = zero

    plane = (rows, LANES)
    lane = lane_of(plane)
    slot = lane % SPAN
    holder = lane // SPAN
    depth = 0.5 + 0.25 * class_ref[...].astype(F32)
    D[0] = depth
    packed_depth = shifted(depth, 8)
    for i in range(1, FOLD):
        packed_depth = jnp.where(holder == i, shifted(depth, 8 + SPAN * i), packed_depth)
    SR[fields] = shifted(packed_depth, -4)
    SL[fields] = shifted(packed_depth, -8)

    pl.semaphore_wait(barrier, 2 + n_dom - 1)

    def send(source, target, there, send_sem, recv_sem):
        return pltpu.make_async_remote_copy(
            src_ref=source,
            dst_ref=target,
            send_sem=send_sem,
            recv_sem=recv_sem,
            device_id=(me_dom, there),
            device_id_type=MESH,
        )

    depth_left = send(SL.at[fields], RR.at[fields], left, depth_send.at[0], depth_recv.at[0])
    depth_right = send(SR.at[fields], RL.at[fields], right, depth_send.at[1], depth_recv.at[1])
    depth_left.start()
    depth_right.start()

    tall = (rows, 3 * rows)
    RT[...] = jnp.maximum(
        0, ROW_REACH + 1 - jnp.abs(row_of(tall) - lane_of(tall) % rows)
    ).astype(F32).astype(BF16)
    wide = (2 * LANES, 2 * LANES)
    to = lane_of(wide)
    have = row_of(wide)
    near = jnp.maximum(0, radius + 1 - jnp.abs(have % LANES - to % LANES))
    WOWN[...] = jnp.where(have // LANES == to // LANES, near, 0).astype(F32).astype(BF16)
    column = have % radius + jnp.where(have < LANES, LANES, -radius)
    near = jnp.maximum(0, radius + 1 - jnp.abs(column - to % LANES))
    WHALO[...] = (
        jnp.where((have % LANES) // radius == to // LANES, near, 0).astype(F32).astype(BF16)
    )

    where = where_ref[...]
    value = value_ref[...]
    count_obs = where.shape[1]
    in_row = row_of((rows, count_obs)) == where // LANES
    in_col = row_of((LANES, count_obs)) == where % LANES
    cols_hot = jnp.where(in_col, 1.0, 0.0).astype(BF16)

    def on_grid(piece):
        left_side = jnp.where(in_row, piece, 0.0).astype(BF16)
        return lax.dot_general(
            left_side, cols_hot, (((1,), (1,)), ((), ())), preferred_element_type=F32
        )

    def on_grid_exact(values):
        a, b, c = pieces(values)
        return on_grid(a.astype(F32)) + (on_grid(b.astype(F32)) + on_grid(c.astype(F32)))

    count = on_grid(jnp.ones_like(value))
    total_obs = on_grid_exact(value)
    squares = on_grid_exact(value * value)
    mean_obs = total_obs / jnp.maximum(count, 1.0)
    OBS[0] = -0.5 * count
    OBS[1] = mean_obs
    OBS[2] = -0.5 * (squares - total_obs * mean_obs)

    for g in range(groups):
        load(g).wait()

        def pack(f, carry, g=g):
            q = shifted(X[g * FOLD, f, pl.ds(PAD, rows), :], 8)
            for i in range(1, FOLD):
                q = jnp.where(
                    holder == i,
                    shifted(X[g * FOLD + i, f, pl.ds(PAD, rows), :], 8 + SPAN * i),
                    q,
                )
            Q[g, f] = q
            return carry

        lax.fori_loop(0, fields, pack, 0)

    def edges(f, carry):
        to_right = shifted(Q[0, f], -4)
        to_left = shifted(Q[0, f], -8)
        for g in range(1, groups):
            mine = slot // 4 == g
            to_right = jnp.where(mine, shifted(Q[g, f], 4 * g - 4), to_right)
            to_left = jnp.where(mine, shifted(Q[g, f], 4 * g - 8), to_left)
        SR[f] = to_right
        SL[f] = to_left
        return carry

    lax.fori_loop(0, fields, edges, 0)
    body = pl.ds(0, fields)
    edge_left = send(SL.at[body], RR.at[body], left, edge_send.at[0], edge_recv.at[0])
    edge_right = send(SR.at[body], RL.at[body], right, edge_send.at[1], edge_recv.at[1])
    edge_left.start()
    edge_right.start()

    def one_step(read, write, d):
        for r in range(0, rows, CHUNK):
            h = read(0, r)
            u = read(1, r)
            v = read(2, r)
            u1 = u - HALF_DT * (east(h) - west(h)) + DT_F * v
            v1 = v - HALF_DT * (read(0, r + 1) - read(0, r - 1)) - DT_F * u
            write(1, r, u1)
            write(2, r, v1)
            deep = D[d, r : r + CHUNK, :]
            du = deep * u1
            DV[PAD + r : PAD + r + CHUNK, :] = deep * v1
            HP[r : r + CHUNK, :] = h - HALF_DT * (east(du) - west(du))
            u2 = HALF_DT * u1
            v2 = HALF_DT * v1
            for f in (3, 4):
                a = read(f, r)
                write(
                    f,
                    r,
                    a - (u2 * (east(a) - west(a)) + v2 * (read(f, r + 1) - read(f, r - 1))),
                )
        for r in range(0, rows, CHUNK):
            up = DV[PAD + r + 1 : PAD + r + 1 + CHUNK, :]
            down = DV[PAD + r - 1 : PAD + r - 1 + CHUNK, :]
            write(0, r, HP[r : r + CHUNK, :] - HALF_DT * (up - down))

    def ahead(m, d):
        def read_x(f, r):
            return X[m, f, PAD + r : PAD + r + CHUNK, :]

        def write_x(f, r, q):
            X[m, f, PAD + r : PAD + r + CHUNK, :] = q

        def read_y(f, r):
            return Y[f, PAD + r : PAD + r + CHUNK, :]

        def write_y(f, r, q):
            Y[f, PAD + r : PAD + r + CHUNK, :] = q

        one_step(read_x, write_y, d)
        one_step(read_y, write_x, d)

    def ahead_main(m, carry):
        ahead(m, 0)
        return carry

    lax.fori_loop(0, members, ahead_main, 0)

    depth_left.wait()
    depth_right.wait()
    D[1] = jnp.where(slot < 8, packed_depth_of(D[0], holder), shifted(RR[fields], 8))
    D[2] = jnp.where(slot >= 8, packed_depth_of(D[0], holder), shifted(RL[fields], 4))
    edge_left.wait()
    edge_right.wait()

    def strips(f, carry):
        for g in range(groups):
            q = Q[g, f]
            X[members + g, f, pl.ds(PAD, rows), :] = jnp.where(
                slot < 8, q, shifted(RR[f], 8 - 4 * g)
            )
            X[members + groups + g, f, pl.ds(PAD, rows), :] = jnp.where(
                slot >= 8, q, shifted(RL[f], 4 - 4 * g)
            )
        return carry

    lax.fori_loop(0, fields, strips, 0)

    def ahead_strip(s, carry):
        ahead(members + s, 1 + s // groups)
        return carry

    lax.fori_loop(0, 2 * groups, ahead_strip, 0)

    def join(f, carry):
        for g in range(groups):
            FE[g, f] = jnp.where(
                slot < 8,
                X[members + g, f, pl.ds(PAD, rows), :],
                X[members + groups + g, f, pl.ds(PAD, rows), :],
            )
        return carry

    lax.fori_loop(0, fields, join, 0)

    at_edge = (lane < 4) | (lane >= LANES - 4)

    def place(i):
        return lax.rem(LANES + LANES - 8 - SPAN * i, LANES)

    def halo_left(p):
        return send(TOL.at[p], HR.at[p], left, halo_send.at[0, p], halo_recv.at[0, p])

    def halo_right(p):
        return send(TOR.at[p], HL.at[p], right, halo_send.at[1, p], halo_recv.at[1, p])

    def likelihood(p, carry):
        both = []
        for k in range(2):
            m = 2 * p + k
            edge = pltpu.roll(FE[m // FOLD, 0], place(lax.rem(m, FOLD)), 1)
            h = jnp.where(at_edge, edge, X[m, 0, pl.ds(PAD, rows), :])
            miss = OBS[1] - h
            both.append(OBS[0] * (miss * miss) + OBS[2])
        a, b, c = pieces(jnp.concatenate(both, axis=1))
        smooth = dot(RT[...], jnp.concatenate([a, b, c], axis=0))
        SM[p] = smooth
        first, second = smooth[:, :LANES], smooth[:, LANES:]
        low = lane < radius
        TOL[p] = jnp.where(low, first, shifted(second, radius))
        TOR[p] = jnp.where(low, shifted(first, radius), second)
        halo_left(p).start()
        halo_right(p).start()
        return carry

    lax.fori_loop(0, pairs, likelihood, 0)

    def columns(q, table):
        a, b, c = pieces(q)
        return dot(a, table) + (dot(b, table) + dot(c, table))

    def own_columns(p, carry):
        PART[p] = columns(SM[p], WOWN[...])
        return carry

    lax.fori_loop(0, pairs, own_columns, 0)

    def halo_wait(p, carry):
        halo_left(p).wait()
        halo_right(p).wait()
        return carry

    lax.fori_loop(0, pairs, halo_wait, 0)

    scale = 1.0 / ((ROW_REACH + 1.0) * (radius + 1.0))
    cut = (share, LANES)
    cut_lane = lane_of(cut)
    cut_edge = (cut_lane < 4) | (cut_lane >= LANES - 4)
    cut_holder = (cut_lane) // SPAN

    def weigh(b, slot_out):
        start = pl.multiple_of(b * share, 8)
        here = pl.ds(start, share)
        there = pl.ds(PAD + start, share)
        halo = jnp.concatenate([HR[:, here, :], HL[:, here, :]], axis=2)
        smooth = PART[:, here, :].reshape(pairs * share, 2 * LANES) + columns(
            halo.reshape(pairs * share, 2 * LANES), WHALO[...]
        )
        smooth = smooth.reshape(pairs, share, 2 * LANES)
        power = anneal_ref[here, :] * scale
        peak = None
        for p in range(pairs):
            for k in range(2):
                logw = power * smooth[p, :, k * LANES : (k + 1) * LANES]
                LW[2 * p + k] = logw
                peak = logw if peak is None else jnp.maximum(peak, logw)
        total = jnp.zeros(cut, F32)
        sums = [jnp.zeros(cut, F32) for _ in range(fields)]
        edge_sums = [jnp.zeros(cut, F32) for _ in range(fields)]
        for g in range(groups):
            packed = None
            for i in range(FOLD):
                m = g * FOLD + i
                w = jnp.exp(LW[m] - peak)
                total = total + w
                for f in range(fields):
                    sums[f] = sums[f] + w * X[m, f, there, :]
                moved = shifted(w, 8 + SPAN * i)
                packed = moved if packed is None else jnp.where(cut_holder == i, moved, packed)
            for f in range(fields):
                edge_sums[f] = edge_sums[f] + packed * FE[g, f, here, :]
        GIVE[slot_out, 0] = peak
        GIVE[slot_out, 1] = total
        for f in range(fields):
            e = edge_sums[f]
            e = e + shifted(e, SPAN)
            e = e + shifted(e, 2 * SPAN)
            e = e + shifted(e, 4 * SPAN)
            GIVE[slot_out, 2 + f] = jnp.where(cut_edge, shifted(e, LANES - 8), sums[f])

    def give(off):
        return pltpu.make_async_remote_copy(
            src_ref=GIVE.at[off],
            dst_ref=TAKE.at[off - 1],
            send_sem=part_send.at[off - 1],
            recv_sem=part_recv.at[off - 1],
            device_id=(lax.rem(me_dom + off, n_dom), me_col),
            device_id_type=MESH,
        )

    def offset(j):
        return 2 + j - 3 * (j // 2)

    def weigh_others(j, carry):
        off = offset(j)
        weigh(lax.rem(me_dom + off, n_dom), off)
        give(off).start()
        return carry

    lax.fori_loop(0, n_dom - 1, weigh_others, 0)
    weigh(me_dom, 0)
    for off in range(1, n_dom):
        give(off).wait()

    peaks = [GIVE[0, 0]] + [TAKE[k, 0] for k in range(n_dom - 1)]
    peak = functools.reduce(jnp.maximum, peaks)
    factors = [jnp.exp(q - peak) for q in peaks]

    def joined(f):
        result = factors[0] * GIVE[0, f]
        for k in range(n_dom - 1):
            result = result + factors[k + 1] * TAKE[k, f]
        return result

    total = joined(1)
    here = pl.ds(pl.multiple_of(me_dom * share, 8), share)
    for f in range(fields):
        out_ref[f, here, :] = joined(2 + f) / total

    def hand_out(off):
        return pltpu.make_async_remote_copy(
            src_ref=out_ref.at[:, here, :],
            dst_ref=out_ref.at[:, here, :],
            send_sem=out_send.at[off - 1],
            recv_sem=out_recv.at[off - 1],
            device_id=(lax.rem(me_dom + off, n_dom), me_col),
            device_id_type=MESH,
        )

    for off in range(1, n_dom):
        hand_out(off).start()
    for off in range(1, n_dom):
        hand_out(off).wait()


def packed_depth_of(depth, holder):
    packed = shifted(depth, 8)
    for i in range(1, FOLD):
        packed = jnp.where(holder == i, shifted(depth, 8 + SPAN * i), packed)
    return packed


def solution(mesh):
    n_dom = mesh.shape["dom"]
    n_col = mesh.shape["col"]

    def on_device(ensemble, depth_class, obs_index, obs_value, annealing_exponents):
        members, fields, rows, lanes = ensemble.shape
        groups = members // FOLD
        pairs = members // 2
        share = rows // n_dom
        tall = rows + 2 * PAD
        vm = pl.BlockSpec(memory_space=pltpu.VMEM)
        dma = pltpu.SemaphoreType.DMA
        return pl.pallas_call(
            functools.partial(kernel, n_dom, n_col),
            out_shape=jax.ShapeDtypeStruct((fields, rows, lanes), F32),
            in_specs=[pl.BlockSpec(memory_space=pl.ANY), vm, vm, vm, vm],
            out_specs=vm,
            scratch_shapes=[
                pltpu.VMEM((members + 2 * groups, fields, tall, lanes), F32),
                pltpu.VMEM((fields, tall, lanes), F32),
                pltpu.VMEM((tall, lanes), F32),
                pltpu.VMEM((rows, lanes), F32),
                pltpu.VMEM((3, rows, lanes), F32),
                pltpu.VMEM((groups, fields, rows, lanes), F32),
                pltpu.VMEM((groups, fields, rows, lanes), F32),
                pltpu.VMEM((fields + 1, rows, lanes), F32),
                pltpu.VMEM((fields + 1, rows, lanes), F32),
                pltpu.VMEM((fields + 1, rows, lanes), F32),
                pltpu.VMEM((fields + 1, rows, lanes), F32),
                pltpu.VMEM((3, rows, lanes), F32),
                pltpu.VMEM((pairs, rows, 2 * lanes), F32),
                pltpu.VMEM((pairs, rows, 2 * lanes), F32),
                pltpu.VMEM((pairs, rows, lanes), F32),
                pltpu.VMEM((pairs, rows, lanes), F32),
                pltpu.VMEM((pairs, rows, lanes), F32),
                pltpu.VMEM((pairs, rows, lanes), F32),
                pltpu.VMEM((members, share, lanes), F32),
                pltpu.VMEM((n_dom, fields + 2, share, lanes), F32),
                pltpu.VMEM((n_dom - 1, fields + 2, share, lanes), F32),
                pltpu.VMEM((rows, 3 * rows), BF16),
                pltpu.VMEM((2 * lanes, 2 * lanes), BF16),
                pltpu.VMEM((2 * lanes, 2 * lanes), BF16),
                dma((groups,)),
                dma((2,)),
                dma((2,)),
                dma((2,)),
                dma((2,)),
                dma((2, pairs)),
                dma((2, pairs)),
                dma((n_dom - 1,)),
                dma((n_dom - 1,)),
                dma((n_dom - 1,)),
                dma((n_dom - 1,)),
            ],
            compiler_params=pltpu.CompilerParams(
                collective_id=0, has_side_effects=True, vmem_limit_bytes=48 * 1024 * 1024
            ),
            cost_estimate=pl.CostEstimate(
                flops=200_000_000, bytes_accessed=9_000_000, transcendentals=400_000
            ),
        )(
            ensemble,
            depth_class,
            obs_index.reshape(1, -1),
            obs_value.reshape(1, -1),
            annealing_exponents,
        )

    in_specs = (P("dom", None, None, "col"), P(None, "col"), P("col"), P("col"), P(None, "col"))
    out_specs = P(None, None, "col")
    return jax.shard_map(
        on_device, mesh=mesh, in_specs=in_specs, out_specs=out_specs, check_vma=False
    )
```

```python
import functools

import jax
import jax.numpy as jnp
from jax import lax
from jax.experimental import pallas as pl
from jax.experimental.pallas import tpu as pltpu
from jax.sharding import PartitionSpec as P

MESH = pl.DeviceIdType.MESH
F32 = jnp.float32
BF16 = jnp.bfloat16

TIME_STEP = 0.25
CORIOLIS = 0.2
HALF_DT = 0.5 * TIME_STEP
DT_F = TIME_STEP * CORIOLIS

ROW_REACH = 8
LANES = 128
PAD = 8
FOLD = 8
SPAN = 16
CHUNK = 32
EARLY = 16


def east(q):
    return pltpu.roll(q, LANES - 1, q.ndim - 1)


def west(q):
    return pltpu.roll(q, 1, q.ndim - 1)


def shifted(q, amount):
    return pltpu.roll(q, amount % LANES, q.ndim - 1)


def pieces(q):
    first = q.astype(BF16)
    rest = q - first.astype(F32)
    second = rest.astype(BF16)
    third = (rest - second.astype(F32)).astype(BF16)
    return first, second, third


def lane_of(shape):
    return lax.broadcasted_iota(jnp.int32, shape, len(shape) - 1)


def row_of(shape):
    return lax.broadcasted_iota(jnp.int32, shape, len(shape) - 2)


def dot(a, b):
    return jnp.dot(a, b, preferred_element_type=F32)


def kernel(
    n_dom,
    n_col,
    ens_ref,
    class_ref,
    where_ref,
    value_ref,
    anneal_ref,
    out_ref,
    X,
    U1,
    Y,
    YT,
    DV,
    HP,
    CLS,
    WHERE,
    VALUE,
    ANNEAL,
    D,
    QD,
    Q,
    FE,
    SL,
    SR,
    RL,
    RR,
    OBS,
    SM,
    PART,
    TOL,
    TOR,
    HL,
    HR,
    LW,
    GIVE,
    TAKE,
    RT,
    WOWN,
    WHALO,
    DX,
    small_sem,
    load_sem,
    edge_send,
    edge_recv,
    halo_send,
    halo_recv,
    part_send,
    part_recv,
    out_send,
    out_recv,
):
    members, fields, rows, _ = ens_ref.shape
    groups = members // FOLD
    pairs = members // 2
    share = rows // n_dom
    radius = LANES // 2
    flow = 3
    me_dom = lax.axis_index("dom")
    me_col = lax.axis_index("col")
    right = lax.rem(me_col + 1, n_col)
    left = lax.rem(me_col + n_col - 1, n_col)
    inner = pl.ds(PAD, rows)

    def load(g, tracers):
        which = pl.ds(flow, fields - flow) if tracers else pl.ds(0, flow)
        return pltpu.make_async_copy(
            ens_ref.at[pl.ds(g * FOLD, FOLD), which],
            X.at[pl.ds(g * FOLD, FOLD), which, inner, :],
            load_sem.at[int(tracers), g],
        )

    small = [
        pltpu.make_async_copy(source, target, small_sem.at[k])
        for k, (source, target) in enumerate(
            ((class_ref, CLS), (where_ref, WHERE), (value_ref, VALUE), (anneal_ref, ANNEAL))
        )
    ]
    load(0, False).start()
    for copy in small:
        copy.start()
    for g in range(1, groups):
        load(g, False).start()
    for g in range(groups):
        load(g, True).start()

    barrier = pltpu.get_barrier_semaphore()
    for other in (left, right):
        pl.semaphore_signal(barrier, inc=1, device_id=(me_dom, other), device_id_type=MESH)
    for off in range(1, n_dom):
        pl.semaphore_signal(
            barrier,
            inc=1,
            device_id=(lax.rem(me_dom + off, n_dom), me_col),
            device_id_type=MESH,
        )

    zero = jnp.zeros((PAD, LANES), F32)

    def clear(m, carry):
        for f in (0, 3, 4):
            X[m, f, 0:PAD, :] = zero
            X[m, f, PAD + rows : PAD + rows + PAD, :] = zero
        return carry

    lax.fori_loop(0, members + 2 * groups, clear, 0)
    for padded in (Y.at[0], YT.at[0], YT.at[1], DV):
        padded[0:PAD, :] = zero
        padded[PAD + rows : PAD + rows + PAD, :] = zero

    tall = (rows, 3 * rows)
    RT[...] = jnp.maximum(
        0, ROW_REACH + 1 - jnp.abs(row_of(tall) - lane_of(tall) % rows)
    ).astype(F32).astype(BF16)
    wide = (2 * LANES, 2 * LANES)
    to = lane_of(wide)
    have = row_of(wide)
    near = jnp.maximum(0, radius + 1 - jnp.abs(have % LANES - to % LANES))
    WOWN[...] = jnp.where(have // LANES == to // LANES, near, 0).astype(F32).astype(BF16)
    column = have % radius + jnp.where(have < LANES, LANES, -radius)
    near = jnp.maximum(0, radius + 1 - jnp.abs(column - to % LANES))
    WHALO[...] = (
        jnp.where((have % LANES) // radius == to // LANES, near, 0).astype(F32).astype(BF16)
    )

    wide = (2 * LANES, LANES)
    ahead_by = (row_of(wide) - lane_of(wide)) % LANES
    DX[...] = (
        jnp.where(ahead_by == 1, HALF_DT, jnp.where(ahead_by == LANES - 1, -HALF_DT, 0.0))
    ).astype(BF16)

    for copy in small:
        copy.wait()

    plane = (rows, LANES)
    lane = lane_of(plane)
    slot = lane % SPAN
    holder = lane // SPAN
    depth = 0.5 + 0.25 * CLS[...].astype(F32)
    D[0] = depth
    packed_depth = shifted(depth, 8)
    for i in range(1, FOLD):
        packed_depth = jnp.where(holder == i, shifted(depth, 8 + SPAN * i), packed_depth)
    QD[...] = packed_depth
    SR[0] = shifted(packed_depth, -4)
    SL[0] = shifted(packed_depth, -8)

    def pack_group(g, first, last):
        def pack(f, carry):
            q = shifted(X[g * FOLD, f, inner, :], 8)
            for i in range(1, FOLD):
                q = jnp.where(
                    holder == i, shifted(X[g * FOLD + i, f, inner, :], 8 + SPAN * i), q
                )
            Q[g, f] = q
            return carry

        lax.fori_loop(first, last, pack, 0)

    def edges(f, carry):
        to_right = shifted(Q[0, f], -4)
        to_left = shifted(Q[0, f], -8)
        for g in range(1, groups):
            mine = slot // 4 == g
            to_right = jnp.where(mine, shifted(Q[g, f], 4 * g - 4), to_right)
            to_left = jnp.where(mine, shifted(Q[g, f], 4 * g - 8), to_left)
        SR[1 + f] = to_right
        SL[1 + f] = to_left
        return carry

    def send(source, target, there, send_sem, recv_sem):
        return pltpu.make_async_remote_copy(
            src_ref=source,
            dst_ref=target,
            send_sem=send_sem,
            recv_sem=recv_sem,
            device_id=(me_dom, there),
            device_id_type=MESH,
        )

    def edge_copies(tracers):
        which = pl.ds(1 + flow, fields - flow) if tracers else pl.ds(0, 1 + flow)
        k = int(tracers)
        return (
            send(SL.at[which], RR.at[which], left, edge_send.at[k, 0], edge_recv.at[k, 0]),
            send(SR.at[which], RL.at[which], right, edge_send.at[k, 1], edge_recv.at[k, 1]),
        )

    for g in range(groups):
        load(g, False).wait()
        pack_group(g, 0, flow)
    lax.fori_loop(0, flow, edges, 0)
    pl.semaphore_wait(barrier, 2 + n_dom - 1)
    flow_edges = edge_copies(False)
    for copy in flow_edges:
        copy.start()

    for g in range(groups):
        load(g, True).wait()
        pack_group(g, flow, fields)
    lax.fori_loop(flow, fields, edges, 0)
    tracer_edges = edge_copies(True)
    for copy in tracer_edges:
        copy.start()

    where = WHERE[...]
    value = VALUE[...]
    parts = where.shape[0]

    def along(q):
        return jnp.concatenate([q[j : j + 1, :] for j in range(parts)], axis=1)

    obs_row = along(where // LANES)
    obs_col = along(where % LANES)
    obs_value = along(value)
    count_obs = parts * LANES
    in_row = row_of((rows, count_obs)) == obs_row
    in_col = row_of((LANES, count_obs)) == obs_col
    cols_hot = jnp.where(in_col, 1.0, 0.0).astype(BF16)

    def on_grid(piece):
        left_side = jnp.where(in_row, piece, 0.0).astype(BF16)
        return lax.dot_general(
            left_side, cols_hot, (((1,), (1,)), ((), ())), preferred_element_type=F32
        )

    def on_grid_exact(values):
        a, b, c = pieces(values)
        return on_grid(a.astype(F32)) + (on_grid(b.astype(F32)) + on_grid(c.astype(F32)))

    count = on_grid(jnp.ones_like(obs_value))
    total_obs = on_grid_exact(obs_value)
    squares = on_grid_exact(obs_value * obs_value)
    mean_obs = total_obs / jnp.maximum(count, 1.0)
    OBS[0] = -0.5 * count
    OBS[1] = mean_obs
    OBS[2] = -0.5 * (squares - total_obs * mean_obs)

    def flow_step(h_ref, u_ref, v_ref, to_h, to_u, to_v, d):
        for r in range(0, rows, CHUNK):
            cut = pl.ds(r, CHUNK)
            mid = pl.ds(PAD + r, CHUNK)
            h = h_ref[mid, :]
            u = u_ref(r)
            v = v_ref(r)
            u1 = u - HALF_DT * (east(h) - west(h)) + DT_F * v
            slope = h_ref[pl.ds(PAD + r + 1, CHUNK), :] - h_ref[pl.ds(PAD + r - 1, CHUNK), :]
            v1 = v - HALF_DT * slope - DT_F * u
            to_u(r, u1)
            to_v(r, v1)
            deep = D[d, cut, :]
            du = deep * u1
            DV[mid, :] = deep * v1
            HP[cut, :] = h - HALF_DT * (east(du) - west(du))
        for r in range(0, rows, CHUNK):
            up = DV[pl.ds(PAD + r + 1, CHUNK), :]
            down = DV[pl.ds(PAD + r - 1, CHUNK), :]
            to_h[pl.ds(PAD + r, CHUNK), :] = HP[pl.ds(r, CHUNK), :] - HALF_DT * (up - down)

    def flow_ahead(m, d):
        def get_x(f):
            return lambda r: X[m, f, pl.ds(PAD + r, CHUNK), :]

        def get_u(f):
            return lambda r: U1[m, f, pl.ds(r, CHUNK), :]

        def put_x(f):
            def put(r, q):
                X[m, f, pl.ds(PAD + r, CHUNK), :] = q

            return put

        def put_u(f):
            def put(r, q):
                U1[m, f, pl.ds(r, CHUNK), :] = q

            return put

        flow_step(X.at[m, 0], get_x(1), get_x(2), Y.at[0], put_u(0), put_u(1), d)
        flow_step(Y.at[0], get_u(0), get_u(1), X.at[m, 0], put_x(1), put_x(2), d)

    def tracers_ahead(m):
        for step in range(2):
            ends = [(X.at[m, f], YT.at[f - flow]) for f in range(flow, fields)]
            if step == 1:
                ends = [(target, source) for source, target in ends]
            split = []
            for source, _ in ends:
                a = source[inner, :]
                first = a.astype(BF16)
                second = (a - first.astype(F32)).astype(BF16)
                split.append(jnp.concatenate([first, second], axis=1))
            across = dot(jnp.concatenate(split, axis=0), DX[...])
            for r in range(0, rows, CHUNK):
                mid = pl.ds(PAD + r, CHUNK)
                if step == 0:
                    u = U1[m, 0, pl.ds(r, CHUNK), :]
                    v = U1[m, 1, pl.ds(r, CHUNK), :]
                else:
                    u = X[m, 1, mid, :]
                    v = X[m, 2, mid, :]
                v = HALF_DT * v
                for k, (source, target) in enumerate(ends):
                    slope = (
                        source[pl.ds(PAD + r + 1, CHUNK), :] - source[pl.ds(PAD + r - 1, CHUNK), :]
                    )
                    steep = across[k * rows + r : k * rows + r + CHUNK, :]
                    target[mid, :] = source[mid, :] - (u * steep + v * slope)

    def flow_main(m, carry):
        flow_ahead(m, 0)
        return carry

    early = EARLY
    lax.fori_loop(0, early, flow_main, 0)

    def strips(f, carry):
        for g in range(groups):
            q = Q[g, f]
            X[members + g, f, inner, :] = jnp.where(slot < 8, q, shifted(RR[1 + f], 8 - 4 * g))
            X[members + groups + g, f, inner, :] = jnp.where(
                slot >= 8, q, shifted(RL[1 + f], 4 - 4 * g)
            )
        return carry

    def join(f, carry):
        for g in range(groups):
            FE[g, f] = jnp.where(
                slot < 8, X[members + g, f, inner, :], X[members + groups + g, f, inner, :]
            )
        return carry

    for copy in flow_edges:
        copy.wait()
    D[1] = jnp.where(slot < 8, QD[...], shifted(RR[0], 8))
    D[2] = jnp.where(slot >= 8, QD[...], shifted(RL[0], 4))
    lax.fori_loop(0, flow, strips, 0)

    def flow_strip(s, carry):
        flow_ahead(members + s, 1 + s // groups)
        return carry

    lax.fori_loop(0, 2 * groups, flow_strip, 0)
    join(0, 0)

    at_edge = (lane < 4) | (lane >= LANES - 4)

    def place(i):
        return lax.rem(LANES + LANES - 8 - SPAN * i, LANES)

    def halo_left(p):
        return send(TOL.at[p], HR.at[p], left, halo_send.at[0, p], halo_recv.at[0, p])

    def halo_right(p):
        return send(TOR.at[p], HL.at[p], right, halo_send.at[1, p], halo_recv.at[1, p])

    def likelihood(p, carry):
        both = []
        for k in range(2):
            m = 2 * p + k
            edge = pltpu.roll(FE[m // FOLD, 0], place(lax.rem(m, FOLD)), 1)
            h = jnp.where(at_edge, edge, X[m, 0, inner, :])
            miss = OBS[1] - h
            both.append(OBS[0] * (miss * miss) + OBS[2])
        a, b, c = pieces(jnp.concatenate(both, axis=1))
        smooth = dot(RT[...], jnp.concatenate([a, b, c], axis=0))
        SM[p] = smooth
        first, second = smooth[:, :LANES], smooth[:, LANES:]
        low = lane < radius
        turned = shifted(jnp.where(low, second, first), radius)
        TOL[p] = jnp.where(low, first, turned)
        TOR[p] = jnp.where(low, turned, second)
        halo_left(p).start()
        halo_right(p).start()
        return carry

    def flow_and_likelihood(p, carry):
        ahead = p + early // 2
        flow_ahead(2 * ahead, 0)
        flow_ahead(2 * ahead + 1, 0)
        return likelihood(p, carry)

    lax.fori_loop(0, pairs - early // 2, flow_and_likelihood, 0)
    lax.fori_loop(pairs - early // 2, pairs, likelihood, 0)

    def tracers_main(m, carry):
        tracers_ahead(m)
        return carry

    for copy in tracer_edges:
        copy.wait()
    lax.fori_loop(flow, fields, strips, 0)
    lax.fori_loop(0, members + 2 * groups, tracers_main, 0, unroll=4)
    lax.fori_loop(1, fields, join, 0)

    def columns(q, table):
        a, b, c = pieces(q)
        return dot(a, table) + (dot(b, table) + dot(c, table))

    def own_columns(p, carry):
        PART[p] = columns(SM[p], WOWN[...])
        return carry

    lax.fori_loop(0, pairs, own_columns, 0, unroll=4)

    def halo_wait(p, carry):
        halo_left(p).wait()
        halo_right(p).wait()
        return carry

    lax.fori_loop(0, pairs, halo_wait, 0)

    scale = 1.0 / ((ROW_REACH + 1.0) * (radius + 1.0))
    cut = (share, LANES)
    cut_lane = lane_of(cut)
    cut_edge = (cut_lane < 4) | (cut_lane >= LANES - 4)
    cut_holder = (cut_lane) // SPAN

    def weigh(b, slot_out):
        start = pl.multiple_of(b * share, 8)
        here = pl.ds(start, share)
        there = pl.ds(PAD + start, share)
        halo = jnp.concatenate([HR[:, here, :], HL[:, here, :]], axis=2)
        smooth = PART[:, here, :].reshape(pairs * share, 2 * LANES) + columns(
            halo.reshape(pairs * share, 2 * LANES), WHALO[...]
        )
        smooth = smooth.reshape(pairs, share, 2 * LANES)
        power = ANNEAL[here, :] * scale
        peak = None
        for p in range(pairs):
            for k in range(2):
                logw = power * smooth[p, :, k * LANES : (k + 1) * LANES]
                LW[2 * p + k] = logw
                peak = logw if peak is None else jnp.maximum(peak, logw)
        total = jnp.zeros(cut, F32)
        sums = [jnp.zeros(cut, F32) for _ in range(fields)]
        edge_sums = [jnp.zeros(cut, F32) for _ in range(fields)]
        for g in range(groups):
            packed = None
            for i in range(FOLD):
                m = g * FOLD + i
                w = jnp.exp(LW[m] - peak)
                total = total + w
                for f in range(fields):
                    sums[f] = sums[f] + w * X[m, f, there, :]
                moved = shifted(w, 8 + SPAN * i)
                packed = moved if packed is None else jnp.where(cut_holder == i, moved, packed)
            for f in range(fields):
                edge_sums[f] = edge_sums[f] + packed * FE[g, f, here, :]
        GIVE[slot_out, 0] = peak
        GIVE[slot_out, 1] = total
        for f in range(fields):
            e = edge_sums[f]
            e = e + shifted(e, SPAN)
            e = e + shifted(e, 2 * SPAN)
            e = e + shifted(e, 4 * SPAN)
            GIVE[slot_out, 2 + f] = jnp.where(cut_edge, shifted(e, LANES - 8), sums[f])

    def give(off):
        return pltpu.make_async_remote_copy(
            src_ref=GIVE.at[off],
            dst_ref=TAKE.at[off - 1],
            send_sem=part_send.at[off - 1],
            recv_sem=part_recv.at[off - 1],
            device_id=(lax.rem(me_dom + off, n_dom), me_col),
            device_id_type=MESH,
        )

    def offset(j):
        return 2 + j - 3 * (j // 2)

    def weigh_others(j, carry):
        off = offset(j)
        weigh(lax.rem(me_dom + off, n_dom), off)
        give(off).start()
        return carry

    lax.fori_loop(0, n_dom - 1, weigh_others, 0)
    weigh(me_dom, 0)
    for off in range(1, n_dom):
        give(off).wait()

    peaks = [GIVE[0, 0]] + [TAKE[k, 0] for k in range(n_dom - 1)]
    peak = functools.reduce(jnp.maximum, peaks)
    factors = [jnp.exp(q - peak) for q in peaks]

    def joined(f):
        result = factors[0] * GIVE[0, f]
        for k in range(n_dom - 1):
            result = result + factors[k + 1] * TAKE[k, f]
        return result

    total = joined(1)
    here = pl.ds(pl.multiple_of(me_dom * share, 8), share)
    for f in range(fields):
        out_ref[f, here, :] = joined(2 + f) / total

    def hand_out(off):
        return pltpu.make_async_remote_copy(
            src_ref=out_ref.at[:, here, :],
            dst_ref=out_ref.at[:, here, :],
            send_sem=out_send.at[off - 1],
            recv_sem=out_recv.at[off - 1],
            device_id=(lax.rem(me_dom + off, n_dom), me_col),
            device_id_type=MESH,
        )

    for off in range(1, n_dom):
        hand_out(off).start()
    for off in range(1, n_dom):
        hand_out(off).wait()


def solution(mesh):
    n_dom = mesh.shape["dom"]
    n_col = mesh.shape["col"]

    def on_device(ensemble, depth_class, obs_index, obs_value, annealing_exponents):
        members, fields, rows, lanes = ensemble.shape
        groups = members // FOLD
        pairs = members // 2
        share = rows // n_dom
        tall = rows + 2 * PAD
        vm = pl.BlockSpec(memory_space=pltpu.VMEM)
        dma = pltpu.SemaphoreType.DMA
        return pl.pallas_call(
            functools.partial(kernel, n_dom, n_col),
            out_shape=jax.ShapeDtypeStruct((fields, rows, lanes), F32),
            in_specs=[pl.BlockSpec(memory_space=pl.ANY)] * 5,
            out_specs=vm,
            scratch_shapes=[
                pltpu.VMEM((members + 2 * groups, fields, tall, lanes), F32),
                pltpu.VMEM((members + 2 * groups, 2, rows, lanes), F32),
                pltpu.VMEM((1, tall, lanes), F32),
                pltpu.VMEM((2, tall, lanes), F32),
                pltpu.VMEM((tall, lanes), F32),
                pltpu.VMEM((rows, lanes), F32),
                pltpu.VMEM((rows, lanes), jnp.int32),
                pltpu.VMEM((obs_index.shape[0] // lanes, lanes), jnp.int32),
                pltpu.VMEM((obs_index.shape[0] // lanes, lanes), F32),
                pltpu.VMEM((rows, lanes), F32),
                pltpu.VMEM((3, rows, lanes), F32),
                pltpu.VMEM((rows, lanes), F32),
                pltpu.VMEM((groups, fields, rows, lanes), F32),
                pltpu.VMEM((groups, fields, rows, lanes), F32),
                pltpu.VMEM((fields + 1, rows, lanes), F32),
                pltpu.VMEM((fields + 1, rows, lanes), F32),
                pltpu.VMEM((fields + 1, rows, lanes), F32),
                pltpu.VMEM((fields + 1, rows, lanes), F32),
                pltpu.VMEM((3, rows, lanes), F32),
                pltpu.VMEM((pairs, rows, 2 * lanes), F32),
                pltpu.VMEM((pairs, rows, 2 * lanes), F32),
                pltpu.VMEM((pairs, rows, lanes), F32),
                pltpu.VMEM((pairs, rows, lanes), F32),
                pltpu.VMEM((pairs, rows, lanes), F32),
                pltpu.VMEM((pairs, rows, lanes), F32),
                pltpu.VMEM((members, share, lanes), F32),
                pltpu.VMEM((n_dom, fields + 2, share, lanes), F32),
                pltpu.VMEM((n_dom - 1, fields + 2, share, lanes), F32),
                pltpu.VMEM((rows, 3 * rows), BF16),
                pltpu.VMEM((2 * lanes, 2 * lanes), BF16),
                pltpu.VMEM((2 * lanes, 2 * lanes), BF16),
                pltpu.VMEM((2 * lanes, lanes), BF16),
                dma((4,)),
                dma((2, groups)),
                dma((2, 2)),
                dma((2, 2)),
                dma((2, pairs)),
                dma((2, pairs)),
                dma((n_dom - 1,)),
                dma((n_dom - 1,)),
                dma((n_dom - 1,)),
                dma((n_dom - 1,)),
            ],
            compiler_params=pltpu.CompilerParams(
                collective_id=0, has_side_effects=True, vmem_limit_bytes=62 * 1024 * 1024
            ),
            cost_estimate=pl.CostEstimate(
                flops=200_000_000, bytes_accessed=9_000_000, transcendentals=400_000
            ),
        )(
            ensemble,
            depth_class,
            obs_index.reshape(-1, lanes),
            obs_value.reshape(-1, lanes),
            annealing_exponents,
        )

    in_specs = (P("dom", None, None, "col"), P(None, "col"), P("col"), P("col"), P(None, "col"))
    out_specs = P(None, None, "col")
    return jax.shard_map(
        on_device, mesh=mesh, in_specs=in_specs, out_specs=out_specs, check_vma=False
    )
```

```python
import functools

import jax
import jax.numpy as jnp
from jax import lax
from jax.experimental import pallas as pl
from jax.experimental.pallas import tpu as pltpu
from jax.sharding import PartitionSpec as P

MESH = pl.DeviceIdType.MESH
F32 = jnp.float32
BF16 = jnp.bfloat16

TIME_STEP = 0.25
CORIOLIS = 0.2
HALF_DT = 0.5 * TIME_STEP
DT_F = TIME_STEP * CORIOLIS

ROW_REACH = 8
LANES = 128
PAD = 8
FOLD = 8
SPAN = 16
CHUNK = 32
EARLY = 12
BESIDE = 4


def shifted(q, amount):
    return pltpu.roll(q, amount % LANES, q.ndim - 1)


def pieces(q):
    first = q.astype(BF16)
    rest = q - first.astype(F32)
    second = rest.astype(BF16)
    third = (rest - second.astype(F32)).astype(BF16)
    return first, second, third


def lane_of(shape):
    return lax.broadcasted_iota(jnp.int32, shape, len(shape) - 1)


def row_of(shape):
    return lax.broadcasted_iota(jnp.int32, shape, len(shape) - 2)


def dot(a, b):
    return jnp.dot(a, b, preferred_element_type=F32)


def kernel(
    n_dom,
    n_col,
    ens_ref,
    class_ref,
    where_ref,
    value_ref,
    anneal_ref,
    out_ref,
    X,
    U1,
    Y,
    YT,
    DV,
    CLS,
    WHERE,
    VALUE,
    ANNEAL,
    D,
    QD,
    Q,
    FE,
    SL,
    SR,
    RL,
    RR,
    OBS,
    SM,
    PART,
    TOL,
    TOR,
    HL,
    HR,
    LW,
    GIVE,
    TAKE,
    RT,
    WOWN,
    WHALO,
    DX,
    small_sem,
    load_sem,
    edge_send,
    edge_recv,
    halo_send,
    halo_recv,
    part_send,
    part_recv,
    out_send,
    out_recv,
):
    members, fields, rows, _ = ens_ref.shape
    groups = members // FOLD
    pairs = members // 2
    share = rows // n_dom
    radius = LANES // 2
    flow = 3
    me_dom = lax.axis_index("dom")
    me_col = lax.axis_index("col")
    right = lax.rem(me_col + 1, n_col)
    left = lax.rem(me_col + n_col - 1, n_col)
    inner = pl.ds(PAD, rows)

    def load(g, tracers):
        which = pl.ds(flow, fields - flow) if tracers else pl.ds(0, flow)
        return pltpu.make_async_copy(
            ens_ref.at[pl.ds(g * FOLD, FOLD), which],
            X.at[pl.ds(g * FOLD, FOLD), which, inner, :],
            load_sem.at[int(tracers), g],
        )

    small = [
        pltpu.make_async_copy(source, target, small_sem.at[k])
        for k, (source, target) in enumerate(
            ((class_ref, CLS), (where_ref, WHERE), (value_ref, VALUE), (anneal_ref, ANNEAL))
        )
    ]
    load(0, False).start()
    for copy in small:
        copy.start()
    for g in range(1, groups):
        load(g, False).start()
    for g in range(groups):
        load(g, True).start()

    barrier = pltpu.get_barrier_semaphore()
    for other in (left, right):
        pl.semaphore_signal(barrier, inc=1, device_id=(me_dom, other), device_id_type=MESH)
    for off in range(1, n_dom):
        pl.semaphore_signal(
            barrier,
            inc=1,
            device_id=(lax.rem(me_dom + off, n_dom), me_col),
            device_id_type=MESH,
        )

    zero = jnp.zeros((PAD, LANES), F32)

    def clear(m, carry):
        for f in (0, 3, 4):
            X[m, f, 0:PAD, :] = zero
            X[m, f, PAD + rows : PAD + rows + PAD, :] = zero
        return carry

    lax.fori_loop(0, members + 2 * groups, clear, 0)
    for k in range(BESIDE):
        for padded in (Y.at[k], DV.at[k], YT.at[k, 0], YT.at[k, 1]):
            padded[0:PAD, :] = zero
            padded[PAD + rows : PAD + rows + PAD, :] = zero

    tall = (rows, 3 * rows)
    RT[...] = jnp.maximum(
        0, ROW_REACH + 1 - jnp.abs(row_of(tall) - lane_of(tall) % rows)
    ).astype(F32).astype(BF16)
    wide = (2 * LANES, 2 * LANES)
    to = lane_of(wide)
    have = row_of(wide)
    near = jnp.maximum(0, radius + 1 - jnp.abs(have % LANES - to % LANES))
    WOWN[...] = jnp.where(have // LANES == to // LANES, near, 0).astype(F32).astype(BF16)
    column = have % radius + jnp.where(have < LANES, LANES, -radius)
    near = jnp.maximum(0, radius + 1 - jnp.abs(column - to % LANES))
    WHALO[...] = (
        jnp.where((have % LANES) // radius == to // LANES, near, 0).astype(F32).astype(BF16)
    )

    wide = (3 * LANES, LANES)
    ahead_by = (row_of(wide) - lane_of(wide)) % LANES
    DX[...] = (
        jnp.where(ahead_by == 1, HALF_DT, jnp.where(ahead_by == LANES - 1, -HALF_DT, 0.0))
    ).astype(BF16)

    for copy in small:
        copy.wait()

    plane = (rows, LANES)
    lane = lane_of(plane)
    slot = lane % SPAN
    holder = lane // SPAN
    depth = 0.5 + 0.25 * CLS[...].astype(F32)
    D[0] = depth
    packed_depth = shifted(depth, 8)
    for i in range(1, FOLD):
        packed_depth = jnp.where(holder == i, shifted(depth, 8 + SPAN * i), packed_depth)
    QD[...] = packed_depth
    def pack_group(g, first, last):
        for f in range(first, last):
            q = shifted(X[g * FOLD, f, inner, :], 8)
            for i in range(1, FOLD):
                q = jnp.where(
                    holder == i, shifted(X[g * FOLD + i, f, inner, :], 8 + SPAN * i), q
                )
            Q[g, f] = q

    def edges(f):
        keep = (slot >= 4) & (slot < 12)
        even = jnp.where(keep, Q[0, f], shifted(Q[1, f], 8))
        odd = shifted(jnp.where(keep, Q[2, f], shifted(Q[3, f], 8)), 4)
        SR[f] = jnp.where(slot % 8 >= 4, even, odd)
        SL[f] = jnp.where(slot % 8 >= 4, odd, even)

    def send(source, target, there, send_sem, recv_sem):
        return pltpu.make_async_remote_copy(
            src_ref=source,
            dst_ref=target,
            send_sem=send_sem,
            recv_sem=recv_sem,
            device_id=(me_dom, there),
            device_id_type=MESH,
        )

    def edge_copies(f):
        to_left, to_right = (QD, QD) if f == fields else (SL.at[f], SR.at[f])
        return (
            send(to_left, RR.at[f], left, edge_send.at[f, 0], edge_recv.at[f, 0]),
            send(to_right, RL.at[f], right, edge_send.at[f, 1], edge_recv.at[f, 1]),
        )

    travelling = [edge_copies(f) for f in range(fields + 1)]
    moved_by = (0, -8, -4, -12)

    def begin(f):
        for copy in travelling[f]:
            copy.start()

    for g in range(groups):
        load(g, False).wait()
        pack_group(g, 0, 1)
    edges(0)
    pl.semaphore_wait(barrier, 2 + n_dom - 1)
    begin(fields)
    begin(0)
    for f in range(1, fields):
        for g in range(groups):
            if f == flow:
                load(g, True).wait()
            pack_group(g, f, f + 1)
        edges(f)
        begin(f)

    where = WHERE[...]
    value = VALUE[...]
    parts = where.shape[0]

    def along(q):
        return jnp.concatenate([q[j : j + 1, :] for j in range(parts)], axis=1)

    obs_row = along(where // LANES)
    obs_col = along(where % LANES)
    obs_value = along(value)
    count_obs = parts * LANES
    in_row = row_of((rows, count_obs)) == obs_row
    in_col = row_of((LANES, count_obs)) == obs_col
    cols_hot = jnp.where(in_col, 1.0, 0.0).astype(BF16)

    def on_grid(piece):
        left_side = jnp.where(in_row, piece, 0.0).astype(BF16)
        return lax.dot_general(
            left_side, cols_hot, (((1,), (1,)), ((), ())), preferred_element_type=F32
        )

    def on_grid_exact(values):
        a, b, c = pieces(values)
        return on_grid(a.astype(F32)) + (on_grid(b.astype(F32)) + on_grid(c.astype(F32)))

    count = on_grid(jnp.ones_like(obs_value))
    total_obs = on_grid_exact(obs_value)
    squares = on_grid_exact(obs_value * obs_value)
    mean_obs = total_obs / jnp.maximum(count, 1.0)
    OBS[0] = -0.5 * count
    OBS[1] = mean_obs
    OBS[2] = -0.5 * (squares - total_obs * mean_obs)

    def split_in(q, count):
        found = []
        for k in range(count):
            found.append(q.astype(BF16))
            if k < count - 1:
                q = q - found[-1].astype(F32)
        return jnp.concatenate(found, axis=1)

    def flow_ahead(ms, d):
        for step in range(2):
            ends = [(X.at[m, 0], Y.at[k]) for k, m in enumerate(ms)]
            if step == 1:
                ends = [(target, source) for source, target in ends]
            across = [dot(split_in(h_ref[inner, :], 3), DX[...]) for h_ref, _ in ends]
            steep = []
            for k, m in enumerate(ms):
                h_ref = ends[k][0]
                split = []
                for r in range(0, rows, CHUNK):
                    cut = pl.ds(r, CHUNK)
                    mid = pl.ds(PAD + r, CHUNK)
                    if step == 0:
                        u, v = X[m, 1, mid, :], X[m, 2, mid, :]
                    else:
                        u, v = U1[m, 0, cut, :], U1[m, 1, cut, :]
                    u1 = u - across[k][r : r + CHUNK, :] + DT_F * v
                    slope = (
                        h_ref[pl.ds(PAD + r + 1, CHUNK), :] - h_ref[pl.ds(PAD + r - 1, CHUNK), :]
                    )
                    v1 = v - HALF_DT * slope - DT_F * u
                    if step == 0:
                        U1[m, 0, cut, :] = u1
                        U1[m, 1, cut, :] = v1
                    else:
                        X[m, 1, mid, :] = u1
                        X[m, 2, mid, :] = v1
                    deep = D[d, cut, :]
                    DV[k, mid, :] = deep * v1
                    split.append(split_in(deep * u1, 3))
                steep.append(dot(jnp.concatenate(split, axis=0), DX[...]))
            for k, m in enumerate(ms):
                h_ref, to_ref = ends[k]
                for r in range(0, rows, CHUNK):
                    mid = pl.ds(PAD + r, CHUNK)
                    slope = DV[k, pl.ds(PAD + r + 1, CHUNK), :] - DV[k, pl.ds(PAD + r - 1, CHUNK), :]
                    to_ref[mid, :] = h_ref[mid, :] - (
                        steep[k][r : r + CHUNK, :] + HALF_DT * slope
                    )

    def tracers_ahead(ms):
        for step in range(2):
            steep = []
            for k, m in enumerate(ms):
                for f in range(flow, fields):
                    source = X.at[m, f] if step == 0 else YT.at[k, f - flow]
                    steep.append(split_in(source[inner, :], 2))
            steep = [
                dot(jnp.concatenate(steep[2 * k : 2 * k + 2], axis=0), DX[0 : 2 * LANES, :])
                for k in range(len(ms))
            ]
            for k, m in enumerate(ms):
                ends = [(X.at[m, f], YT.at[k, f - flow]) for f in range(flow, fields)]
                if step == 1:
                    ends = [(target, source) for source, target in ends]
                for r in range(0, rows, CHUNK):
                    mid = pl.ds(PAD + r, CHUNK)
                    if step == 0:
                        u = U1[m, 0, pl.ds(r, CHUNK), :]
                        v = U1[m, 1, pl.ds(r, CHUNK), :]
                    else:
                        u = X[m, 1, mid, :]
                        v = X[m, 2, mid, :]
                    v = HALF_DT * v
                    for j, (source, target) in enumerate(ends):
                        slope = (
                            source[pl.ds(PAD + r + 1, CHUNK), :]
                            - source[pl.ds(PAD + r - 1, CHUNK), :]
                        )
                        across = steep[k][j * rows + r : j * rows + r + CHUNK, :]
                        target[mid, :] = source[mid, :] - (u * across + v * slope)

    def some(first):
        return [first + k for k in range(BESIDE)]

    def flow_main(m, carry):
        flow_ahead(some(BESIDE * m), 0)
        return carry

    early = EARLY
    lax.fori_loop(0, early // BESIDE, flow_main, 0)

    def strips(f, carry):
        for g in range(groups):
            q = Q[g, f]
            X[members + g, f, inner, :] = jnp.where(slot < 8, q, shifted(RR[f], moved_by[g]))
            X[members + groups + g, f, inner, :] = jnp.where(
                slot >= 8, q, shifted(RL[f], moved_by[g])
            )
        return carry

    def join(f, carry):
        for g in range(groups):
            FE[g, f] = jnp.where(
                slot < 8, X[members + g, f, inner, :], X[members + groups + g, f, inner, :]
            )
        return carry

    for f in (fields, 0, 1, 2):
        for copy in travelling[f]:
            copy.wait()
    D[1] = jnp.where(slot < 8, QD[...], RR[fields])
    D[2] = jnp.where(slot >= 8, QD[...], RL[fields])
    lax.fori_loop(0, flow, strips, 0)

    def flow_strip(s, carry):
        flow_ahead(some(members + BESIDE * s), 1 + BESIDE * s // groups)
        return carry

    lax.fori_loop(0, 2 * groups // BESIDE, flow_strip, 0)
    join(0, 0)

    at_edge = (lane < 4) | (lane >= LANES - 4)

    def place(i):
        return lax.rem(LANES + LANES - 8 - SPAN * i, LANES)

    def halo_left(p):
        return send(TOL.at[p], HR.at[p], left, halo_send.at[0, p], halo_recv.at[0, p])

    def halo_right(p):
        return send(TOR.at[p], HL.at[p], right, halo_send.at[1, p], halo_recv.at[1, p])

    def likelihood(ps):
        logs = []
        for p in ps:
            both = []
            for k in range(2):
                m = 2 * p + k
                edge = pltpu.roll(FE[m // FOLD, 0], place(lax.rem(m, FOLD)), 1)
                h = jnp.where(at_edge, edge, X[m, 0, inner, :])
                miss = OBS[1] - h
                both.append(OBS[0] * (miss * miss) + OBS[2])
            logs.append(jnp.concatenate(both, axis=1))
        smoothed = [dot(RT[...], jnp.concatenate(pieces(q), axis=0)) for q in logs]
        for p, smooth in zip(ps, smoothed):
            SM[p] = smooth
            first, second = smooth[:, :LANES], smooth[:, LANES:]
            low = lane < radius
            turned = shifted(jnp.where(low, second, first), radius)
            TOL[p] = jnp.where(low, first, turned)
            TOR[p] = jnp.where(low, turned, second)
            halo_left(p).start()
            halo_right(p).start()

    def flow_and_likelihood(q, carry):
        flow_ahead(some(BESIDE * q + early), 0)
        likelihood([2 * q, 2 * q + 1])
        return carry

    def only_likelihood(q, carry):
        likelihood([2 * q, 2 * q + 1])
        return carry

    both_ways = (members - early) // BESIDE
    lax.fori_loop(0, both_ways, flow_and_likelihood, 0)
    lax.fori_loop(both_ways, pairs // 2, only_likelihood, 0)

    def tracers_main(m, carry):
        tracers_ahead(some(BESIDE * m))
        return carry

    for f in range(flow, fields):
        for copy in travelling[f]:
            copy.wait()
    lax.fori_loop(flow, fields, strips, 0)
    lax.fori_loop(0, (members + 2 * groups) // BESIDE, tracers_main, 0)
    lax.fori_loop(1, fields, join, 0)

    def columns(q, table):
        a, b, c = pieces(q)
        return dot(a, table) + (dot(b, table) + dot(c, table))

    def own_columns(p, carry):
        PART[p] = columns(SM[p], WOWN[...])
        return carry

    lax.fori_loop(0, pairs, own_columns, 0, unroll=4)

    def halo_wait(p, carry):
        halo_left(p).wait()
        halo_right(p).wait()
        return carry

    lax.fori_loop(0, pairs, halo_wait, 0)

    scale = 1.0 / ((ROW_REACH + 1.0) * (radius + 1.0))
    cut = (share, LANES)
    cut_lane = lane_of(cut)
    cut_edge = (cut_lane < 4) | (cut_lane >= LANES - 4)
    cut_holder = (cut_lane) // SPAN

    def weigh(b, slot_out):
        start = pl.multiple_of(b * share, 8)
        here = pl.ds(start, share)
        there = pl.ds(PAD + start, share)
        halo = jnp.concatenate([HR[:, here, :], HL[:, here, :]], axis=2)
        smooth = PART[:, here, :].reshape(pairs * share, 2 * LANES) + columns(
            halo.reshape(pairs * share, 2 * LANES), WHALO[...]
        )
        smooth = smooth.reshape(pairs, share, 2 * LANES)
        power = ANNEAL[here, :] * scale
        peak = None
        for p in range(pairs):
            for k in range(2):
                logw = power * smooth[p, :, k * LANES : (k + 1) * LANES]
                LW[2 * p + k] = logw
                peak = logw if peak is None else jnp.maximum(peak, logw)
        total = jnp.zeros(cut, F32)
        sums = [jnp.zeros(cut, F32) for _ in range(fields)]
        edge_sums = [jnp.zeros(cut, F32) for _ in range(fields)]
        for g in range(groups):
            packed = None
            for i in range(FOLD):
                m = g * FOLD + i
                w = jnp.exp(LW[m] - peak)
                total = total + w
                for f in range(fields):
                    sums[f] = sums[f] + w * X[m, f, there, :]
                moved = shifted(w, 8 + SPAN * i)
                packed = moved if packed is None else jnp.where(cut_holder == i, moved, packed)
            for f in range(fields):
                edge_sums[f] = edge_sums[f] + packed * FE[g, f, here, :]
        GIVE[slot_out, 0] = peak
        GIVE[slot_out, 1] = total
        for f in range(fields):
            e = edge_sums[f]
            e = e + shifted(e, SPAN)
            e = e + shifted(e, 2 * SPAN)
            e = e + shifted(e, 4 * SPAN)
            GIVE[slot_out, 2 + f] = jnp.where(cut_edge, shifted(e, LANES - 8), sums[f])

    def give(off):
        return pltpu.make_async_remote_copy(
            src_ref=GIVE.at[off],
            dst_ref=TAKE.at[off - 1],
            send_sem=part_send.at[off - 1],
            recv_sem=part_recv.at[off - 1],
            device_id=(lax.rem(me_dom + off, n_dom), me_col),
            device_id_type=MESH,
        )

    def offset(j):
        return 2 + j - 3 * (j // 2)

    def weigh_others(j, carry):
        off = offset(j)
        weigh(lax.rem(me_dom + off, n_dom), off)
        give(off).start()
        return carry

    lax.fori_loop(0, n_dom - 1, weigh_others, 0)
    weigh(me_dom, 0)
    for off in range(1, n_dom):
        give(off).wait()

    peaks = [GIVE[0, 0]] + [TAKE[k, 0] for k in range(n_dom - 1)]
    peak = functools.reduce(jnp.maximum, peaks)
    factors = [jnp.exp(q - peak) for q in peaks]

    def joined(f):
        result = factors[0] * GIVE[0, f]
        for k in range(n_dom - 1):
            result = result + factors[k + 1] * TAKE[k, f]
        return result

    total = joined(1)
    here = pl.ds(pl.multiple_of(me_dom * share, 8), share)
    for f in range(fields):
        out_ref[f, here, :] = joined(2 + f) / total

    def hand_out(off):
        return pltpu.make_async_remote_copy(
            src_ref=out_ref.at[:, here, :],
            dst_ref=out_ref.at[:, here, :],
            send_sem=out_send.at[off - 1],
            recv_sem=out_recv.at[off - 1],
            device_id=(lax.rem(me_dom + off, n_dom), me_col),
            device_id_type=MESH,
        )

    for off in range(1, n_dom):
        hand_out(off).start()
    for off in range(1, n_dom):
        hand_out(off).wait()


def solution(mesh):
    n_dom = mesh.shape["dom"]
    n_col = mesh.shape["col"]

    def on_device(ensemble, depth_class, obs_index, obs_value, annealing_exponents):
        members, fields, rows, lanes = ensemble.shape
        groups = members // FOLD
        pairs = members // 2
        share = rows // n_dom
        tall = rows + 2 * PAD
        vm = pl.BlockSpec(memory_space=pltpu.VMEM)
        dma = pltpu.SemaphoreType.DMA
        return pl.pallas_call(
            functools.partial(kernel, n_dom, n_col),
            out_shape=jax.ShapeDtypeStruct((fields, rows, lanes), F32),
            in_specs=[pl.BlockSpec(memory_space=pl.ANY)] * 5,
            out_specs=vm,
            scratch_shapes=[
                pltpu.VMEM((members + 2 * groups, fields, tall, lanes), F32),
                pltpu.VMEM((members + 2 * groups, 2, rows, lanes), F32),
                pltpu.VMEM((BESIDE, tall, lanes), F32),
                pltpu.VMEM((BESIDE, 2, tall, lanes), F32),
                pltpu.VMEM((BESIDE, tall, lanes), F32),
                pltpu.VMEM((rows, lanes), jnp.int32),
                pltpu.VMEM((obs_index.shape[0] // lanes, lanes), jnp.int32),
                pltpu.VMEM((obs_index.shape[0] // lanes, lanes), F32),
                pltpu.VMEM((rows, lanes), F32),
                pltpu.VMEM((3, rows, lanes), F32),
                pltpu.VMEM((rows, lanes), F32),
                pltpu.VMEM((groups, fields, rows, lanes), F32),
                pltpu.VMEM((groups, fields, rows, lanes), F32),
                pltpu.VMEM((fields, rows, lanes), F32),
                pltpu.VMEM((fields, rows, lanes), F32),
                pltpu.VMEM((fields + 1, rows, lanes), F32),
                pltpu.VMEM((fields + 1, rows, lanes), F32),
                pltpu.VMEM((3, rows, lanes), F32),
                pltpu.VMEM((pairs, rows, 2 * lanes), F32),
                pltpu.VMEM((pairs, rows, 2 * lanes), F32),
                pltpu.VMEM((pairs, rows, lanes), F32),
                pltpu.VMEM((pairs, rows, lanes), F32),
                pltpu.VMEM((pairs, rows, lanes), F32),
                pltpu.VMEM((pairs, rows, lanes), F32),
                pltpu.VMEM((members, share, lanes), F32),
                pltpu.VMEM((n_dom, fields + 2, share, lanes), F32),
                pltpu.VMEM((n_dom - 1, fields + 2, share, lanes), F32),
                pltpu.VMEM((rows, 3 * rows), BF16),
                pltpu.VMEM((2 * lanes, 2 * lanes), BF16),
                pltpu.VMEM((2 * lanes, 2 * lanes), BF16),
                pltpu.VMEM((3 * lanes, lanes), BF16),
                dma((4,)),
                dma((2, groups)),
                dma((fields + 1, 2)),
                dma((fields + 1, 2)),
                dma((2, pairs)),
                dma((2, pairs)),
                dma((n_dom - 1,)),
                dma((n_dom - 1,)),
                dma((n_dom - 1,)),
                dma((n_dom - 1,)),
            ],
            compiler_params=pltpu.CompilerParams(
                collective_id=0, has_side_effects=True, vmem_limit_bytes=62 * 1024 * 1024
            ),
            cost_estimate=pl.CostEstimate(
                flops=200_000_000, bytes_accessed=9_000_000, transcendentals=400_000
            ),
        )(
            ensemble,
            depth_class,
            obs_index.reshape(-1, lanes),
            obs_value.reshape(-1, lanes),
            annealing_exponents,
        )

    in_specs = (P("dom", None, None, "col"), P(None, "col"), P("col"), P("col"), P(None, "col"))
    out_specs = P(None, None, "col")
    return jax.shard_map(
        on_device, mesh=mesh, in_specs=in_specs, out_specs=out_specs, check_vma=False
    )
```

```python
import functools

import jax
import jax.numpy as jnp
from jax import lax
from jax.experimental import pallas as pl
from jax.experimental.pallas import tpu as pltpu
from jax.sharding import PartitionSpec as P

MESH = pl.DeviceIdType.MESH
F32 = jnp.float32
BF16 = jnp.bfloat16

TIME_STEP = 0.25
CORIOLIS = 0.2
HALF_DT = 0.5 * TIME_STEP
DT_F = TIME_STEP * CORIOLIS

ROW_REACH = 8
LANES = 128
PAD = 8
FOLD = 8
SPAN = 16
CHUNK = 32
EARLY = 12
BESIDE = 4
HALF_BAND = 16


def shifted(q, amount):
    return pltpu.roll(q, amount % LANES, q.ndim - 1)


def pieces(q):
    first = q.astype(BF16)
    rest = q - first.astype(F32)
    second = rest.astype(BF16)
    third = (rest - second.astype(F32)).astype(BF16)
    return first, second, third


def lane_of(shape):
    return lax.broadcasted_iota(jnp.int32, shape, len(shape) - 1)


def row_of(shape):
    return lax.broadcasted_iota(jnp.int32, shape, len(shape) - 2)


def dot(a, b):
    return jnp.dot(a, b, preferred_element_type=F32)


def kernel(
    n_dom,
    n_col,
    ens_ref,
    class_ref,
    where_ref,
    value_ref,
    anneal_ref,
    out_ref,
    X,
    U1,
    Y,
    YT,
    DV,
    CLS,
    WHERE,
    VALUE,
    ANNEAL,
    D,
    QD,
    Q,
    FE,
    SL,
    SR,
    RL,
    RR,
    OBS,
    SM,
    PART,
    TOL,
    TOR,
    HL,
    HR,
    LW,
    GIVE,
    TAKE,
    DONE,
    FETCHED,
    RT,
    WOWN,
    WHALO,
    DX,
    small_sem,
    load_sem,
    edge_send,
    edge_recv,
    halo_send,
    halo_recv,
    part_send,
    part_recv,
    out_send,
    out_recv,
):
    members, fields, rows, _ = ens_ref.shape
    groups = members // FOLD
    pairs = members // 2
    share = 8
    band = share * n_dom
    radius = LANES // 2
    flow = 3
    me_dom = lax.axis_index("dom")
    me_col = lax.axis_index("col")
    right = lax.rem(me_col + 1, n_col)
    left = lax.rem(me_col + n_col - 1, n_col)
    inner = pl.ds(PAD, rows)

    def load(g, tracers):
        which = pl.ds(flow, fields - flow) if tracers else pl.ds(0, flow)
        return pltpu.make_async_copy(
            ens_ref.at[pl.ds(g * FOLD, FOLD), which],
            X.at[pl.ds(g * FOLD, FOLD), which, inner, :],
            load_sem.at[int(tracers), g],
        )

    small = [
        pltpu.make_async_copy(source, target, small_sem.at[k])
        for k, (source, target) in enumerate(
            ((class_ref, CLS), (where_ref, WHERE), (value_ref, VALUE), (anneal_ref, ANNEAL))
        )
    ]
    load(0, False).start()
    for copy in small:
        copy.start()
    for g in range(1, groups):
        load(g, False).start()
    for g in range(groups):
        load(g, True).start()

    barrier = pltpu.get_barrier_semaphore()
    for other in (left, right):
        pl.semaphore_signal(barrier, inc=1, device_id=(me_dom, other), device_id_type=MESH)
    for off in range(1, n_dom):
        pl.semaphore_signal(
            barrier,
            inc=1,
            device_id=(lax.rem(me_dom + off, n_dom), me_col),
            device_id_type=MESH,
        )

    zero = jnp.zeros((PAD, LANES), F32)

    def clear(m, carry):
        for f in (0, 3, 4):
            X[m, f, 0:PAD, :] = zero
            X[m, f, PAD + rows : PAD + rows + PAD, :] = zero
        return carry

    lax.fori_loop(0, members + 2 * groups, clear, 0)
    for k in range(BESIDE):
        for padded in (Y.at[k], DV.at[k], YT.at[k, 0], YT.at[k, 1]):
            padded[0:PAD, :] = zero
            padded[PAD + rows : PAD + rows + PAD, :] = zero

    tall = (rows, 3 * rows)
    RT[...] = jnp.maximum(
        0, ROW_REACH + 1 - jnp.abs(row_of(tall) - lane_of(tall) % rows)
    ).astype(F32).astype(BF16)
    wide = (2 * LANES, 2 * LANES)
    to = lane_of(wide)
    have = row_of(wide)
    near = jnp.maximum(0, radius + 1 - jnp.abs(have % LANES - to % LANES))
    WOWN[...] = jnp.where(have // LANES == to // LANES, near, 0).astype(F32).astype(BF16)
    column = have % radius + jnp.where(have < LANES, LANES, -radius)
    near = jnp.maximum(0, radius + 1 - jnp.abs(column - to % LANES))
    WHALO[...] = (
        jnp.where((have % LANES) // radius == to // LANES, near, 0).astype(F32).astype(BF16)
    )

    wide = (3 * LANES, LANES)
    ahead_by = (row_of(wide) - lane_of(wide)) % LANES
    DX[...] = (
        jnp.where(ahead_by == 1, HALF_DT, jnp.where(ahead_by == LANES - 1, -HALF_DT, 0.0))
    ).astype(BF16)

    for copy in small:
        copy.wait()

    plane = (rows, LANES)
    lane = lane_of(plane)
    slot = lane % SPAN
    holder = lane // SPAN
    depth = 0.5 + 0.25 * CLS[...].astype(F32)
    D[0] = depth
    packed_depth = shifted(depth, 8)
    for i in range(1, FOLD):
        packed_depth = jnp.where(holder == i, shifted(depth, 8 + SPAN * i), packed_depth)
    QD[...] = packed_depth
    def pack_group(g, first, last):
        for f in range(first, last):
            q = shifted(X[g * FOLD, f, inner, :], 8)
            for i in range(1, FOLD):
                q = jnp.where(
                    holder == i, shifted(X[g * FOLD + i, f, inner, :], 8 + SPAN * i), q
                )
            Q[g, f] = q

    def edges(f):
        keep = (slot >= 4) & (slot < 12)
        even = jnp.where(keep, Q[0, f], shifted(Q[1, f], 8))
        odd = shifted(jnp.where(keep, Q[2, f], shifted(Q[3, f], 8)), 4)
        SR[f] = jnp.where(slot % 8 >= 4, even, odd)
        SL[f] = jnp.where(slot % 8 >= 4, odd, even)

    def send(source, target, there, send_sem, recv_sem):
        return pltpu.make_async_remote_copy(
            src_ref=source,
            dst_ref=target,
            send_sem=send_sem,
            recv_sem=recv_sem,
            device_id=(me_dom, there),
            device_id_type=MESH,
        )

    def edge_copies(f):
        to_left, to_right = (QD, QD) if f == fields else (SL.at[f], SR.at[f])
        return (
            send(to_left, RR.at[f], left, edge_send.at[f, 0], edge_recv.at[f, 0]),
            send(to_right, RL.at[f], right, edge_send.at[f, 1], edge_recv.at[f, 1]),
        )

    travelling = [edge_copies(f) for f in range(fields + 1)]
    moved_by = (0, -8, -4, -12)

    def begin(f):
        for copy in travelling[f]:
            copy.start()

    for g in range(groups):
        load(g, False).wait()
        pack_group(g, 0, 1)
    edges(0)
    pl.semaphore_wait(barrier, 2 + n_dom - 1)
    begin(fields)
    begin(0)
    for f in range(1, fields):
        for g in range(groups):
            if f == flow:
                load(g, True).wait()
            pack_group(g, f, f + 1)
        edges(f)
        begin(f)

    where = WHERE[...]
    value = VALUE[...]
    parts = where.shape[0]

    def along(q):
        return jnp.concatenate([q[j : j + 1, :] for j in range(parts)], axis=1)

    obs_row = along(where // LANES)
    obs_col = along(where % LANES)
    obs_value = along(value)
    count_obs = parts * LANES
    in_row = row_of((rows, count_obs)) == obs_row
    in_col = row_of((LANES, count_obs)) == obs_col
    cols_hot = jnp.where(in_col, 1.0, 0.0).astype(BF16)

    def on_grid(piece):
        left_side = jnp.where(in_row, piece, 0.0).astype(BF16)
        return lax.dot_general(
            left_side, cols_hot, (((1,), (1,)), ((), ())), preferred_element_type=F32
        )

    def on_grid_exact(values):
        a, b, c = pieces(values)
        return on_grid(a.astype(F32)) + (on_grid(b.astype(F32)) + on_grid(c.astype(F32)))

    count = on_grid(jnp.ones_like(obs_value))
    total_obs = on_grid_exact(obs_value)
    squares = on_grid_exact(obs_value * obs_value)
    mean_obs = total_obs / jnp.maximum(count, 1.0)
    OBS[0] = -0.5 * count
    OBS[1] = mean_obs
    OBS[2] = -0.5 * (squares - total_obs * mean_obs)

    def split_in(q, count):
        found = []
        for k in range(count):
            found.append(q.astype(BF16))
            if k < count - 1:
                q = q - found[-1].astype(F32)
        return jnp.concatenate(found, axis=1)

    def flow_ahead(ms, d):
        for step in range(2):
            ends = [(X.at[m, 0], Y.at[k]) for k, m in enumerate(ms)]
            if step == 1:
                ends = [(target, source) for source, target in ends]
            across = [dot(split_in(h_ref[inner, :], 3), DX[...]) for h_ref, _ in ends]
            steep = []
            for k, m in enumerate(ms):
                h_ref = ends[k][0]
                split = []
                for r in range(0, rows, CHUNK):
                    cut = pl.ds(r, CHUNK)
                    mid = pl.ds(PAD + r, CHUNK)
                    if step == 0:
                        u, v = X[m, 1, mid, :], X[m, 2, mid, :]
                    else:
                        u, v = U1[m, 0, cut, :], U1[m, 1, cut, :]
                    u1 = u - across[k][r : r + CHUNK, :] + DT_F * v
                    slope = (
                        h_ref[pl.ds(PAD + r + 1, CHUNK), :] - h_ref[pl.ds(PAD + r - 1, CHUNK), :]
                    )
                    v1 = v - HALF_DT * slope - DT_F * u
                    if step == 0:
                        U1[m, 0, cut, :] = u1
                        U1[m, 1, cut, :] = v1
                    else:
                        X[m, 1, mid, :] = u1
                        X[m, 2, mid, :] = v1
                    deep = D[d, cut, :]
                    DV[k, mid, :] = deep * v1
                    split.append(split_in(deep * u1, 3))
                steep.append(dot(jnp.concatenate(split, axis=0), DX[...]))
            for k, m in enumerate(ms):
                h_ref, to_ref = ends[k]
                for r in range(0, rows, CHUNK):
                    mid = pl.ds(PAD + r, CHUNK)
                    slope = DV[k, pl.ds(PAD + r + 1, CHUNK), :] - DV[k, pl.ds(PAD + r - 1, CHUNK), :]
                    to_ref[mid, :] = h_ref[mid, :] - (
                        steep[k][r : r + CHUNK, :] + HALF_DT * slope
                    )

    def tracers_ahead(ms):
        for step in range(2):
            steep = []
            for k, m in enumerate(ms):
                for f in range(flow, fields):
                    source = X.at[m, f] if step == 0 else YT.at[k, f - flow]
                    steep.append(split_in(source[inner, :], 2))
            steep = [
                dot(jnp.concatenate(steep[2 * k : 2 * k + 2], axis=0), DX[0 : 2 * LANES, :])
                for k in range(len(ms))
            ]
            for k, m in enumerate(ms):
                ends = [(X.at[m, f], YT.at[k, f - flow]) for f in range(flow, fields)]
                if step == 1:
                    ends = [(target, source) for source, target in ends]
                for r in range(0, rows, CHUNK):
                    mid = pl.ds(PAD + r, CHUNK)
                    if step == 0:
                        u = U1[m, 0, pl.ds(r, CHUNK), :]
                        v = U1[m, 1, pl.ds(r, CHUNK), :]
                    else:
                        u = X[m, 1, mid, :]
                        v = X[m, 2, mid, :]
                    v = HALF_DT * v
                    for j, (source, target) in enumerate(ends):
                        slope = (
                            source[pl.ds(PAD + r + 1, CHUNK), :]
                            - source[pl.ds(PAD + r - 1, CHUNK), :]
                        )
                        across = steep[k][j * rows + r : j * rows + r + CHUNK, :]
                        target[mid, :] = source[mid, :] - (u * across + v * slope)

    def some(first):
        return [first + k for k in range(BESIDE)]

    def flow_main(m, carry):
        flow_ahead(some(BESIDE * m), 0)
        return carry

    early = EARLY
    lax.fori_loop(0, early // BESIDE, flow_main, 0)

    def strips(f, carry):
        for g in range(groups):
            q = Q[g, f]
            X[members + g, f, inner, :] = jnp.where(slot < 8, q, shifted(RR[f], moved_by[g]))
            X[members + groups + g, f, inner, :] = jnp.where(
                slot >= 8, q, shifted(RL[f], moved_by[g])
            )
        return carry

    def join(f, carry):
        for g in range(groups):
            FE[g, f] = jnp.where(
                slot < 8, X[members + g, f, inner, :], X[members + groups + g, f, inner, :]
            )
        return carry

    for f in (fields, 0, 1, 2):
        for copy in travelling[f]:
            copy.wait()
    D[1] = jnp.where(slot < 8, QD[...], RR[fields])
    D[2] = jnp.where(slot >= 8, QD[...], RL[fields])
    lax.fori_loop(0, flow, strips, 0)

    def flow_strip(s, carry):
        flow_ahead(some(members + BESIDE * s), 1 + BESIDE * s // groups)
        return carry

    lax.fori_loop(0, 2 * groups // BESIDE, flow_strip, 0)
    join(0, 0)

    at_edge = (lane < 4) | (lane >= LANES - 4)

    def place(i):
        return lax.rem(LANES + LANES - 8 - SPAN * i, LANES)

    upper = rows - band

    def halo_pair(p):
        here = pl.ds(0, upper)
        return (
            send(TOL.at[p, here], HR.at[p, here], left, halo_send.at[0, p], halo_recv.at[0, p]),
            send(TOR.at[p, here], HL.at[p, here], right, halo_send.at[1, p], halo_recv.at[1, p]),
        )

    def halo_rest():
        here = pl.ds(upper, band)
        return (
            send(
                TOL.at[:, here], HR.at[:, here], left, halo_send.at[0, pairs], halo_recv.at[0, pairs]
            ),
            send(
                TOR.at[:, here], HL.at[:, here], right, halo_send.at[1, pairs], halo_recv.at[1, pairs]
            ),
        )

    def likelihood(ps):
        logs = []
        for p in ps:
            both = []
            for k in range(2):
                m = 2 * p + k
                edge = pltpu.roll(FE[m // FOLD, 0], place(lax.rem(m, FOLD)), 1)
                h = jnp.where(at_edge, edge, X[m, 0, inner, :])
                miss = OBS[1] - h
                both.append(OBS[0] * (miss * miss) + OBS[2])
            logs.append(jnp.concatenate(both, axis=1))
        smoothed = [dot(RT[...], jnp.concatenate(pieces(q), axis=0)) for q in logs]
        for p, smooth in zip(ps, smoothed):
            SM[p] = smooth
            first, second = smooth[:, :LANES], smooth[:, LANES:]
            low = lane < radius
            turned = shifted(jnp.where(low, second, first), radius)
            TOL[p] = jnp.where(low, first, turned)
            TOR[p] = jnp.where(low, turned, second)
            for copy in halo_pair(p):
                copy.start()

    def flow_and_likelihood(q, carry):
        flow_ahead(some(BESIDE * q + early), 0)
        likelihood([2 * q, 2 * q + 1])
        return carry

    def only_likelihood(q, carry):
        likelihood([2 * q, 2 * q + 1])
        return carry

    both_ways = (members - early) // BESIDE
    lax.fori_loop(0, both_ways, flow_and_likelihood, 0)
    lax.fori_loop(both_ways, pairs // 2, only_likelihood, 0)
    for copy in halo_rest():
        copy.start()

    def tracers_main(m, carry):
        tracers_ahead(some(BESIDE * m))
        return carry

    for f in range(flow, fields):
        for copy in travelling[f]:
            copy.wait()
    lax.fori_loop(flow, fields, strips, 0)
    lax.fori_loop(0, (members + 2 * groups) // BESIDE, tracers_main, 0)
    lax.fori_loop(1, fields, join, 0)

    def columns(q, table):
        a, b, c = pieces(q)
        return dot(a, table) + (dot(b, table) + dot(c, table))

    def own_columns(p, carry):
        PART[p] = columns(SM[p], WOWN[...])
        return carry

    lax.fori_loop(0, pairs, own_columns, 0, unroll=4)

    def halo_wait(p, carry):
        for copy in halo_pair(p):
            copy.wait()
        return carry

    scale = 1.0 / ((ROW_REACH + 1.0) * (radius + 1.0))
    cut = (HALF_BAND, LANES)
    cut_lane = lane_of(cut)
    cut_edge = (cut_lane < 4) | (cut_lane >= LANES - 4)
    cut_holder = cut_lane // SPAN

    def weigh(b):
        here = pl.ds(b * band, band)
        halo = jnp.concatenate([HR[:, here, :], HL[:, here, :]], axis=2)
        smooth = PART[:, here, :].reshape(pairs * band, 2 * LANES) + columns(
            halo.reshape(pairs * band, 2 * LANES), WHALO[...]
        )
        smooth = smooth.reshape(pairs, band, 2 * LANES)
        power = ANNEAL[here, :] * scale
        peak = None
        for p in range(pairs):
            for k in range(2):
                logw = power * smooth[p, :, k * LANES : (k + 1) * LANES]
                LW[2 * p + k] = logw
                peak = logw if peak is None else jnp.maximum(peak, logw)
        def set_out(f, start, q):
            for d in range(start // share, (start + q.shape[0]) // share):
                GIVE[b, d, f] = q[d * share - start : (d + 1) * share - start, :]

        set_out(0, 0, peak)
        for start in range(0, band, HALF_BAND):
            within = pl.ds(start, HALF_BAND)
            here = pl.ds(b * band + start, HALF_BAND)
            there = pl.ds(PAD + b * band + start, HALF_BAND)
            best = peak[start : start + HALF_BAND, :]
            total = jnp.zeros(cut, F32)
            sums = [jnp.zeros(cut, F32) for _ in range(fields)]
            edge_sums = [jnp.zeros(cut, F32) for _ in range(fields)]
            for g in range(groups):
                packed = None
                for i in range(FOLD):
                    m = g * FOLD + i
                    w = jnp.exp(LW[m, within, :] - best)
                    total = total + w
                    for f in range(fields):
                        sums[f] = sums[f] + w * X[m, f, there, :]
                    moved = shifted(w, 8 + SPAN * i)
                    packed = moved if packed is None else jnp.where(cut_holder == i, moved, packed)
                for f in range(fields):
                    edge_sums[f] = edge_sums[f] + packed * FE[g, f, here, :]
            set_out(1, start, total)
            for f in range(fields):
                e = edge_sums[f]
                e = e + shifted(e, SPAN)
                e = e + shifted(e, 2 * SPAN)
                e = e + shifted(e, 4 * SPAN)
                set_out(2 + f, start, jnp.where(cut_edge, shifted(e, LANES - 8), sums[f]))

    def give(b, off):
        owner = lax.rem(me_dom + off, n_dom)
        return pltpu.make_async_remote_copy(
            src_ref=GIVE.at[b, owner],
            dst_ref=TAKE.at[b, off - 1],
            send_sem=part_send.at[b, off - 1],
            recv_sem=part_recv.at[b, off - 1],
            device_id=(owner, me_col),
            device_id_type=MESH,
        )

    def hand_out(b, off):
        return pltpu.make_async_remote_copy(
            src_ref=DONE.at[b],
            dst_ref=FETCHED.at[b, off - 1],
            send_sem=out_send.at[b, off - 1],
            recv_sem=out_recv.at[b, off - 1],
            device_id=(lax.rem(me_dom + off, n_dom), me_col),
            device_id_type=MESH,
        )

    far_first = (2, 1, 3)

    def join_band(b):
        for off in far_first:
            give(b, off).wait()
        peaks = [GIVE[b, me_dom, 0]] + [TAKE[b, k, 0] for k in range(n_dom - 1)]
        peak = functools.reduce(jnp.maximum, peaks)
        factors = [jnp.exp(q - peak) for q in peaks]

        def joined(f):
            result = factors[0] * GIVE[b, me_dom, f]
            for k in range(n_dom - 1):
                result = result + factors[k + 1] * TAKE[b, k, f]
            return result

        total = joined(1)
        for f in range(fields):
            DONE[b, f] = joined(2 + f) / total
        for off in far_first:
            hand_out(b, off).start()

    bands = rows // band
    lax.fori_loop(0, pairs, halo_wait, 0)
    for b in range(bands):
        if b == bands - 1:
            for copy in halo_rest():
                copy.wait()
        weigh(b)
        for off in far_first:
            give(b, off).start()
    for b in range(bands):
        join_band(b)
    def place_rows(b, d, source):
        here = pl.ds(pl.multiple_of(b * band + d * share, 8), share)
        for f in range(fields):
            out_ref[f, here, :] = source[f]

    for b in range(bands):
        place_rows(b, me_dom, DONE.at[b])
        for off in far_first:
            hand_out(b, off).wait()
            place_rows(b, lax.rem(me_dom + n_dom - off, n_dom), FETCHED.at[b, off - 1])


def solution(mesh):
    n_dom = mesh.shape["dom"]
    n_col = mesh.shape["col"]

    def on_device(ensemble, depth_class, obs_index, obs_value, annealing_exponents):
        members, fields, rows, lanes = ensemble.shape
        groups = members // FOLD
        pairs = members // 2
        share = 8
        band = share * n_dom
        bands = rows // band
        tall = rows + 2 * PAD
        vm = pl.BlockSpec(memory_space=pltpu.VMEM)
        dma = pltpu.SemaphoreType.DMA
        return pl.pallas_call(
            functools.partial(kernel, n_dom, n_col),
            out_shape=jax.ShapeDtypeStruct((fields, rows, lanes), F32),
            in_specs=[pl.BlockSpec(memory_space=pl.ANY)] * 5,
            out_specs=vm,
            scratch_shapes=[
                pltpu.VMEM((members + 2 * groups, fields, tall, lanes), F32),
                pltpu.VMEM((members + 2 * groups, 2, rows, lanes), F32),
                pltpu.VMEM((BESIDE, tall, lanes), F32),
                pltpu.VMEM((BESIDE, 2, tall, lanes), F32),
                pltpu.VMEM((BESIDE, tall, lanes), F32),
                pltpu.VMEM((rows, lanes), jnp.int32),
                pltpu.VMEM((obs_index.shape[0] // lanes, lanes), jnp.int32),
                pltpu.VMEM((obs_index.shape[0] // lanes, lanes), F32),
                pltpu.VMEM((rows, lanes), F32),
                pltpu.VMEM((3, rows, lanes), F32),
                pltpu.VMEM((rows, lanes), F32),
                pltpu.VMEM((groups, fields, rows, lanes), F32),
                pltpu.VMEM((groups, fields, rows, lanes), F32),
                pltpu.VMEM((fields, rows, lanes), F32),
                pltpu.VMEM((fields, rows, lanes), F32),
                pltpu.VMEM((fields + 1, rows, lanes), F32),
                pltpu.VMEM((fields + 1, rows, lanes), F32),
                pltpu.VMEM((3, rows, lanes), F32),
                pltpu.VMEM((pairs, rows, 2 * lanes), F32),
                pltpu.VMEM((pairs, rows, 2 * lanes), F32),
                pltpu.VMEM((pairs, rows, lanes), F32),
                pltpu.VMEM((pairs, rows, lanes), F32),
                pltpu.VMEM((pairs, rows, lanes), F32),
                pltpu.VMEM((pairs, rows, lanes), F32),
                pltpu.VMEM((members, band, lanes), F32),
                pltpu.VMEM((bands, n_dom, fields + 2, share, lanes), F32),
                pltpu.VMEM((bands, n_dom - 1, fields + 2, share, lanes), F32),
                pltpu.VMEM((bands, fields, share, lanes), F32),
                pltpu.VMEM((bands, n_dom - 1, fields, share, lanes), F32),
                pltpu.VMEM((rows, 3 * rows), BF16),
                pltpu.VMEM((2 * lanes, 2 * lanes), BF16),
                pltpu.VMEM((2 * lanes, 2 * lanes), BF16),
                pltpu.VMEM((3 * lanes, lanes), BF16),
                dma((4,)),
                dma((2, groups)),
                dma((fields + 1, 2)),
                dma((fields + 1, 2)),
                dma((2, pairs + 1)),
                dma((2, pairs + 1)),
                dma((bands, n_dom - 1)),
                dma((bands, n_dom - 1)),
                dma((bands, n_dom - 1)),
                dma((bands, n_dom - 1)),
            ],
            compiler_params=pltpu.CompilerParams(
                collective_id=0, has_side_effects=True, vmem_limit_bytes=62 * 1024 * 1024
            ),
            cost_estimate=pl.CostEstimate(
                flops=200_000_000, bytes_accessed=9_000_000, transcendentals=400_000
            ),
        )(
            ensemble,
            depth_class,
            obs_index.reshape(-1, lanes),
            obs_value.reshape(-1, lanes),
            annealing_exponents,
        )

    in_specs = (P("dom", None, None, "col"), P(None, "col"), P("col"), P("col"), P(None, "col"))
    out_specs = P(None, None, "col")
    return jax.shard_map(
        on_device, mesh=mesh, in_specs=in_specs, out_specs=out_specs, check_vma=False
    )
```

```python
import functools

import jax
import jax.numpy as jnp
from jax import lax
from jax.experimental import pallas as pl
from jax.experimental.pallas import tpu as pltpu
from jax.sharding import PartitionSpec as P

MESH = pl.DeviceIdType.MESH
F32 = jnp.float32
BF16 = jnp.bfloat16

TIME_STEP = 0.25
CORIOLIS = 0.2
HALF_DT = 0.5 * TIME_STEP
DT_F = TIME_STEP * CORIOLIS

ROW_REACH = 8
LANES = 128
PAD = 8
FOLD = 8
SPAN = 16
CHUNK = 32
EARLY = 16
BESIDE = 4
HALF_BAND = 16


def shifted(q, amount):
    return pltpu.roll(q, amount % LANES, q.ndim - 1)


def pieces(q):
    first = q.astype(BF16)
    rest = q - first.astype(F32)
    second = rest.astype(BF16)
    third = (rest - second.astype(F32)).astype(BF16)
    return first, second, third


def lane_of(shape):
    return lax.broadcasted_iota(jnp.int32, shape, len(shape) - 1)


def row_of(shape):
    return lax.broadcasted_iota(jnp.int32, shape, len(shape) - 2)


def dot(a, b):
    return jnp.dot(a, b, preferred_element_type=F32)


def kernel(
    n_dom,
    n_col,
    ens_ref,
    class_ref,
    where_ref,
    value_ref,
    anneal_ref,
    out_ref,
    X,
    U1,
    Y,
    YT,
    DV,
    CLS,
    WHERE,
    VALUE,
    ANNEAL,
    D,
    QD,
    Q,
    FE,
    SL,
    SR,
    RL,
    RR,
    OBS,
    SM,
    PART,
    TOL,
    TOR,
    HL,
    HR,
    LW,
    GIVE,
    TAKE,
    DONE,
    FETCHED,
    RT,
    WOWN,
    WHALO,
    DX,
    small_sem,
    load_sem,
    edge_send,
    edge_recv,
    halo_send,
    halo_recv,
    part_send,
    part_recv,
    out_send,
    out_recv,
):
    members, fields, rows, _ = ens_ref.shape
    groups = members // FOLD
    pairs = members // 2
    share = 8
    band = share * n_dom
    radius = LANES // 2
    flow = 3
    me_dom = lax.axis_index("dom")
    me_col = lax.axis_index("col")
    right = lax.rem(me_col + 1, n_col)
    left = lax.rem(me_col + n_col - 1, n_col)
    inner = pl.ds(PAD, rows)

    def load(g, tracers):
        which = pl.ds(flow, fields - flow) if tracers else pl.ds(0, flow)
        return pltpu.make_async_copy(
            ens_ref.at[pl.ds(g * FOLD, FOLD), which],
            X.at[pl.ds(g * FOLD, FOLD), which, inner, :],
            load_sem.at[int(tracers), g],
        )

    small = [
        pltpu.make_async_copy(source, target, small_sem.at[k])
        for k, (source, target) in enumerate(
            ((class_ref, CLS), (where_ref, WHERE), (value_ref, VALUE), (anneal_ref, ANNEAL))
        )
    ]
    load(0, False).start()
    for copy in small:
        copy.start()
    for g in range(1, groups):
        load(g, False).start()
    for g in range(groups):
        load(g, True).start()

    barrier = pltpu.get_barrier_semaphore()
    for other in (left, right):
        pl.semaphore_signal(barrier, inc=1, device_id=(me_dom, other), device_id_type=MESH)
    for off in range(1, n_dom):
        pl.semaphore_signal(
            barrier,
            inc=1,
            device_id=(lax.rem(me_dom + off, n_dom), me_col),
            device_id_type=MESH,
        )

    zero = jnp.zeros((PAD, LANES), F32)

    def clear(m, carry):
        for f in (0, 3, 4):
            X[m, f, 0:PAD, :] = zero
            X[m, f, PAD + rows : PAD + rows + PAD, :] = zero
        return carry

    lax.fori_loop(0, members + 2 * groups, clear, 0)
    for k in range(BESIDE):
        for padded in (Y.at[k], DV.at[k], YT.at[k, 0], YT.at[k, 1]):
            padded[0:PAD, :] = zero
            padded[PAD + rows : PAD + rows + PAD, :] = zero

    for copy in small:
        copy.wait()

    plane = (rows, LANES)
    lane = lane_of(plane)
    slot = lane % SPAN
    holder = lane // SPAN
    depth = 0.5 + 0.25 * CLS[...].astype(F32)
    D[0] = depth
    packed_depth = shifted(depth, 8)
    for i in range(1, FOLD):
        packed_depth = jnp.where(holder == i, shifted(depth, 8 + SPAN * i), packed_depth)
    QD[...] = packed_depth
    def pack_group(g, first, last):
        for f in range(first, last):
            q = shifted(X[g * FOLD, f, inner, :], 8)
            for i in range(1, FOLD):
                q = jnp.where(
                    holder == i, shifted(X[g * FOLD + i, f, inner, :], 8 + SPAN * i), q
                )
            Q[g, f] = q

    def edges(f):
        keep = (slot >= 4) & (slot < 12)
        even = jnp.where(keep, Q[0, f], shifted(Q[1, f], 8))
        odd = shifted(jnp.where(keep, Q[2, f], shifted(Q[3, f], 8)), 4)
        SR[f] = jnp.where(slot % 8 >= 4, even, odd)
        SL[f] = jnp.where(slot % 8 >= 4, odd, even)

    def send(source, target, there, send_sem, recv_sem):
        return pltpu.make_async_remote_copy(
            src_ref=source,
            dst_ref=target,
            send_sem=send_sem,
            recv_sem=recv_sem,
            device_id=(me_dom, there),
            device_id_type=MESH,
        )

    def edge_copies(f):
        to_left, to_right = (QD, QD) if f == fields else (SL.at[f], SR.at[f])
        return (
            send(to_left, RR.at[f], left, edge_send.at[f, 0], edge_recv.at[f, 0]),
            send(to_right, RL.at[f], right, edge_send.at[f, 1], edge_recv.at[f, 1]),
        )

    travelling = [edge_copies(f) for f in range(fields + 1)]
    moved_by = (0, -8, -4, -12)

    def begin(f):
        for copy in travelling[f]:
            copy.start()

    for g in range(groups):
        load(g, False).wait()
        pack_group(g, 0, 1)
    edges(0)
    pl.semaphore_wait(barrier, 2 + n_dom - 1)
    begin(fields)
    begin(0)
    for f in range(1, fields):
        for g in range(groups):
            if f == flow:
                load(g, True).wait()
            pack_group(g, f, f + 1)
        edges(f)
        begin(f)

    tall = (rows, 3 * rows)
    RT[...] = jnp.maximum(
        0, ROW_REACH + 1 - jnp.abs(row_of(tall) - lane_of(tall) % rows)
    ).astype(F32).astype(BF16)
    wide = (2 * LANES, 2 * LANES)
    to = lane_of(wide)
    have = row_of(wide)
    near = jnp.maximum(0, radius + 1 - jnp.abs(have % LANES - to % LANES))
    WOWN[...] = jnp.where(have // LANES == to // LANES, near, 0).astype(F32).astype(BF16)
    column = have % radius + jnp.where(have < LANES, LANES, -radius)
    near = jnp.maximum(0, radius + 1 - jnp.abs(column - to % LANES))
    WHALO[...] = (
        jnp.where((have % LANES) // radius == to // LANES, near, 0).astype(F32).astype(BF16)
    )

    wide = (3 * LANES, LANES)
    ahead_by = (row_of(wide) - lane_of(wide)) % LANES
    DX[...] = (
        jnp.where(ahead_by == 1, HALF_DT, jnp.where(ahead_by == LANES - 1, -HALF_DT, 0.0))
    ).astype(BF16)

    where = WHERE[...]
    value = VALUE[...]
    parts = where.shape[0]

    def along(q):
        return jnp.concatenate([q[j : j + 1, :] for j in range(parts)], axis=1)

    obs_row = along(where // LANES)
    obs_col = along(where % LANES)
    obs_value = along(value)
    count_obs = parts * LANES
    in_row = row_of((rows, count_obs)) == obs_row
    in_col = row_of((LANES, count_obs)) == obs_col
    cols_hot = jnp.where(in_col, 1.0, 0.0).astype(BF16)

    def on_grid(piece):
        left_side = jnp.where(in_row, piece, 0.0).astype(BF16)
        return lax.dot_general(
            left_side, cols_hot, (((1,), (1,)), ((), ())), preferred_element_type=F32
        )

    def on_grid_exact(values):
        a, b, c = pieces(values)
        return on_grid(a.astype(F32)) + (on_grid(b.astype(F32)) + on_grid(c.astype(F32)))

    count = on_grid(jnp.ones_like(obs_value))
    total_obs = on_grid_exact(obs_value)
    squares = on_grid_exact(obs_value * obs_value)
    mean_obs = total_obs / jnp.maximum(count, 1.0)
    OBS[0] = -0.5 * count
    OBS[1] = mean_obs
    OBS[2] = -0.5 * (squares - total_obs * mean_obs)

    def split_in(q, count):
        found = []
        for k in range(count):
            found.append(q.astype(BF16))
            if k < count - 1:
                q = q - found[-1].astype(F32)
        return jnp.concatenate(found, axis=1)

    def flow_ahead(ms, d):
        for step in range(2):
            ends = [(X.at[m, 0], Y.at[k]) for k, m in enumerate(ms)]
            if step == 1:
                ends = [(target, source) for source, target in ends]
            across = [dot(split_in(h_ref[inner, :], 3), DX[...]) for h_ref, _ in ends]
            steep = []
            for k, m in enumerate(ms):
                h_ref = ends[k][0]
                split = []
                for r in range(0, rows, CHUNK):
                    cut = pl.ds(r, CHUNK)
                    mid = pl.ds(PAD + r, CHUNK)
                    if step == 0:
                        u, v = X[m, 1, mid, :], X[m, 2, mid, :]
                    else:
                        u, v = U1[m, 0, cut, :], U1[m, 1, cut, :]
                    u1 = u - across[k][r : r + CHUNK, :] + DT_F * v
                    slope = (
                        h_ref[pl.ds(PAD + r + 1, CHUNK), :] - h_ref[pl.ds(PAD + r - 1, CHUNK), :]
                    )
                    v1 = v - HALF_DT * slope - DT_F * u
                    if step == 0:
                        U1[m, 0, cut, :] = u1
                        U1[m, 1, cut, :] = v1
                    else:
                        X[m, 1, mid, :] = u1
                        X[m, 2, mid, :] = v1
                    deep = D[d, cut, :]
                    DV[k, mid, :] = deep * v1
                    split.append(split_in(deep * u1, 3))
                steep.append(dot(jnp.concatenate(split, axis=0), DX[...]))
            for k, m in enumerate(ms):
                h_ref, to_ref = ends[k]
                for r in range(0, rows, CHUNK):
                    mid = pl.ds(PAD + r, CHUNK)
                    slope = DV[k, pl.ds(PAD + r + 1, CHUNK), :] - DV[k, pl.ds(PAD + r - 1, CHUNK), :]
                    to_ref[mid, :] = h_ref[mid, :] - (
                        steep[k][r : r + CHUNK, :] + HALF_DT * slope
                    )

    def tracers_ahead(ms):
        for step in range(2):
            steep = []
            for k, m in enumerate(ms):
                for f in range(flow, fields):
                    source = X.at[m, f] if step == 0 else YT.at[k, f - flow]
                    steep.append(split_in(source[inner, :], 2))
            steep = [
                dot(jnp.concatenate(steep[2 * k : 2 * k + 2], axis=0), DX[0 : 2 * LANES, :])
                for k in range(len(ms))
            ]
            for k, m in enumerate(ms):
                ends = [(X.at[m, f], YT.at[k, f - flow]) for f in range(flow, fields)]
                if step == 1:
                    ends = [(target, source) for source, target in ends]
                for r in range(0, rows, CHUNK):
                    mid = pl.ds(PAD + r, CHUNK)
                    if step == 0:
                        u = U1[m, 0, pl.ds(r, CHUNK), :]
                        v = U1[m, 1, pl.ds(r, CHUNK), :]
                    else:
                        u = X[m, 1, mid, :]
                        v = X[m, 2, mid, :]
                    v = HALF_DT * v
                    for j, (source, target) in enumerate(ends):
                        slope = (
                            source[pl.ds(PAD + r + 1, CHUNK), :]
                            - source[pl.ds(PAD + r - 1, CHUNK), :]
                        )
                        across = steep[k][j * rows + r : j * rows + r + CHUNK, :]
                        target[mid, :] = source[mid, :] - (u * across + v * slope)

    def some(first):
        return [first + k for k in range(BESIDE)]

    def flow_main(m, carry):
        flow_ahead(some(BESIDE * m), 0)
        return carry

    early = EARLY
    lax.fori_loop(0, early // BESIDE, flow_main, 0)

    def strips(f, carry):
        for g in range(groups):
            q = Q[g, f]
            X[members + g, f, inner, :] = jnp.where(slot < 8, q, shifted(RR[f], moved_by[g]))
            X[members + groups + g, f, inner, :] = jnp.where(
                slot >= 8, q, shifted(RL[f], moved_by[g])
            )
        return carry

    def join(f, carry):
        for g in range(groups):
            FE[g, f] = jnp.where(
                slot < 8, X[members + g, f, inner, :], X[members + groups + g, f, inner, :]
            )
        return carry

    for f in (fields, 0, 1, 2):
        for copy in travelling[f]:
            copy.wait()
    D[1] = jnp.where(slot < 8, QD[...], RR[fields])
    D[2] = jnp.where(slot >= 8, QD[...], RL[fields])
    lax.fori_loop(0, flow, strips, 0)

    def flow_strip(s, carry):
        flow_ahead(some(members + BESIDE * s), 1 + BESIDE * s // groups)
        return carry

    lax.fori_loop(0, 2 * groups // BESIDE, flow_strip, 0)
    join(0, 0)

    at_edge = (lane < 4) | (lane >= LANES - 4)

    def place(i):
        return lax.rem(LANES + LANES - 8 - SPAN * i, LANES)

    upper = rows - band

    def halo_pair(p):
        here = pl.ds(0, upper)
        return (
            send(TOL.at[p, here], HR.at[p, here], left, halo_send.at[0, p], halo_recv.at[0, p]),
            send(TOR.at[p, here], HL.at[p, here], right, halo_send.at[1, p], halo_recv.at[1, p]),
        )

    def halo_rest():
        here = pl.ds(upper, band)
        return (
            send(
                TOL.at[:, here], HR.at[:, here], left, halo_send.at[0, pairs], halo_recv.at[0, pairs]
            ),
            send(
                TOR.at[:, here], HL.at[:, here], right, halo_send.at[1, pairs], halo_recv.at[1, pairs]
            ),
        )

    def likelihood(ps):
        logs = []
        for p in ps:
            both = []
            for k in range(2):
                m = 2 * p + k
                edge = pltpu.roll(FE[m // FOLD, 0], place(lax.rem(m, FOLD)), 1)
                h = jnp.where(at_edge, edge, X[m, 0, inner, :])
                miss = OBS[1] - h
                both.append(OBS[0] * (miss * miss) + OBS[2])
            logs.append(jnp.concatenate(both, axis=1))
        smoothed = [dot(RT[...], jnp.concatenate(pieces(q), axis=0)) for q in logs]
        for p, smooth in zip(ps, smoothed):
            SM[p] = smooth
            first, second = smooth[:, :LANES], smooth[:, LANES:]
            low = lane < radius
            turned = shifted(jnp.where(low, second, first), radius)
            TOL[p] = jnp.where(low, first, turned)
            TOR[p] = jnp.where(low, turned, second)
            for copy in halo_pair(p):
                copy.start()

    def flow_and_likelihood(q, carry):
        flow_ahead(some(BESIDE * q + early), 0)
        likelihood([2 * q + 2, 2 * q + 3])
        return carry

    def only_likelihood(q, carry):
        likelihood([2 * q, 2 * q + 1])
        return carry

    both_ways = (members - early) // BESIDE
    likelihood([0, 1])
    lax.fori_loop(0, both_ways, flow_and_likelihood, 0)
    lax.fori_loop(both_ways + 1, pairs // 2, only_likelihood, 0)
    for copy in halo_rest():
        copy.start()

    def tracers_main(m, carry):
        tracers_ahead(some(BESIDE * m))
        return carry

    for f in range(flow, fields):
        for copy in travelling[f]:
            copy.wait()
    lax.fori_loop(flow, fields, strips, 0)
    lax.fori_loop(0, (members + 2 * groups) // BESIDE, tracers_main, 0)
    lax.fori_loop(1, fields, join, 0)

    def columns(q, table):
        a, b, c = pieces(q)
        return dot(a, table) + (dot(b, table) + dot(c, table))

    def own_columns(p, carry):
        PART[p] = columns(SM[p], WOWN[...])
        return carry

    lax.fori_loop(0, pairs, own_columns, 0, unroll=4)

    def halo_wait(p, carry):
        for copy in halo_pair(p):
            copy.wait()
        return carry

    scale = 1.0 / ((ROW_REACH + 1.0) * (radius + 1.0))
    cut = (HALF_BAND, LANES)
    cut_lane = lane_of(cut)
    cut_edge = (cut_lane < 4) | (cut_lane >= LANES - 4)
    cut_holder = cut_lane // SPAN

    def weigh(b):
        here = pl.ds(b * band, band)
        halo = jnp.concatenate([HR[:, here, :], HL[:, here, :]], axis=2)
        smooth = PART[:, here, :].reshape(pairs * band, 2 * LANES) + columns(
            halo.reshape(pairs * band, 2 * LANES), WHALO[...]
        )
        smooth = smooth.reshape(pairs, band, 2 * LANES)
        power = ANNEAL[here, :] * scale
        peak = None
        for p in range(pairs):
            for k in range(2):
                logw = power * smooth[p, :, k * LANES : (k + 1) * LANES]
                LW[2 * p + k] = logw
                peak = logw if peak is None else jnp.maximum(peak, logw)
        def set_out(f, start, q):
            for d in range(start // share, (start + q.shape[0]) // share):
                GIVE[b, d, f] = q[d * share - start : (d + 1) * share - start, :]

        set_out(0, 0, peak)
        for start in range(0, band, HALF_BAND):
            within = pl.ds(start, HALF_BAND)
            here = pl.ds(b * band + start, HALF_BAND)
            there = pl.ds(PAD + b * band + start, HALF_BAND)
            best = peak[start : start + HALF_BAND, :]
            total = jnp.zeros(cut, F32)
            sums = [jnp.zeros(cut, F32) for _ in range(fields)]
            edge_sums = [jnp.zeros(cut, F32) for _ in range(fields)]
            for g in range(groups):
                packed = None
                for i in range(FOLD):
                    m = g * FOLD + i
                    w = jnp.exp(LW[m, within, :] - best)
                    total = total + w
                    for f in range(fields):
                        sums[f] = sums[f] + w * X[m, f, there, :]
                    moved = shifted(w, 8 + SPAN * i)
                    packed = moved if packed is None else jnp.where(cut_holder == i, moved, packed)
                for f in range(fields):
                    edge_sums[f] = edge_sums[f] + packed * FE[g, f, here, :]
            set_out(1, start, total)
            for f in range(fields):
                e = edge_sums[f]
                e = e + shifted(e, SPAN)
                e = e + shifted(e, 2 * SPAN)
                e = e + shifted(e, 4 * SPAN)
                set_out(2 + f, start, jnp.where(cut_edge, shifted(e, LANES - 8), sums[f]))

    def give(b, off):
        owner = lax.rem(me_dom + off, n_dom)
        return pltpu.make_async_remote_copy(
            src_ref=GIVE.at[b, owner],
            dst_ref=TAKE.at[b, off - 1],
            send_sem=part_send.at[b, off - 1],
            recv_sem=part_recv.at[b, off - 1],
            device_id=(owner, me_col),
            device_id_type=MESH,
        )

    def hand_out(b, off):
        return pltpu.make_async_remote_copy(
            src_ref=DONE.at[b],
            dst_ref=FETCHED.at[b, off - 1],
            send_sem=out_send.at[b, off - 1],
            recv_sem=out_recv.at[b, off - 1],
            device_id=(lax.rem(me_dom + off, n_dom), me_col),
            device_id_type=MESH,
        )

    far_first = (2, 1, 3)

    def join_band(b):
        for off in far_first:
            give(b, off).wait()
        peaks = [GIVE[b, me_dom, 0]] + [TAKE[b, k, 0] for k in range(n_dom - 1)]
        peak = functools.reduce(jnp.maximum, peaks)
        factors = [jnp.exp(q - peak) for q in peaks]

        def joined(f):
            result = factors[0] * GIVE[b, me_dom, f]
            for k in range(n_dom - 1):
                result = result + factors[k + 1] * TAKE[b, k, f]
            return result

        total = joined(1)
        for f in range(fields):
            DONE[b, f] = joined(2 + f) / total
        for off in far_first:
            hand_out(b, off).start()

    bands = rows // band
    lax.fori_loop(0, pairs, halo_wait, 0)
    for b in range(bands):
        if b == bands - 1:
            for copy in halo_rest():
                copy.wait()
        weigh(b)
        for off in far_first:
            give(b, off).start()
    for b in range(bands):
        join_band(b)
    def place_rows(b, d, source):
        here = pl.ds(pl.multiple_of(b * band + d * share, 8), share)
        for f in range(fields):
            out_ref[f, here, :] = source[f]

    for b in range(bands):
        place_rows(b, me_dom, DONE.at[b])
        for off in far_first:
            hand_out(b, off).wait()
            place_rows(b, lax.rem(me_dom + n_dom - off, n_dom), FETCHED.at[b, off - 1])


def solution(mesh):
    n_dom = mesh.shape["dom"]
    n_col = mesh.shape["col"]

    def on_device(ensemble, depth_class, obs_index, obs_value, annealing_exponents):
        members, fields, rows, lanes = ensemble.shape
        groups = members // FOLD
        pairs = members // 2
        share = 8
        band = share * n_dom
        bands = rows // band
        tall = rows + 2 * PAD
        vm = pl.BlockSpec(memory_space=pltpu.VMEM)
        dma = pltpu.SemaphoreType.DMA
        return pl.pallas_call(
            functools.partial(kernel, n_dom, n_col),
            out_shape=jax.ShapeDtypeStruct((fields, rows, lanes), F32),
            in_specs=[pl.BlockSpec(memory_space=pl.ANY)] * 5,
            out_specs=vm,
            scratch_shapes=[
                pltpu.VMEM((members + 2 * groups, fields, tall, lanes), F32),
                pltpu.VMEM((members + 2 * groups, 2, rows, lanes), F32),
                pltpu.VMEM((BESIDE, tall, lanes), F32),
                pltpu.VMEM((BESIDE, 2, tall, lanes), F32),
                pltpu.VMEM((BESIDE, tall, lanes), F32),
                pltpu.VMEM((rows, lanes), jnp.int32),
                pltpu.VMEM((obs_index.shape[0] // lanes, lanes), jnp.int32),
                pltpu.VMEM((obs_index.shape[0] // lanes, lanes), F32),
                pltpu.VMEM((rows, lanes), F32),
                pltpu.VMEM((3, rows, lanes), F32),
                pltpu.VMEM((rows, lanes), F32),
                pltpu.VMEM((groups, fields, rows, lanes), F32),
                pltpu.VMEM((groups, fields, rows, lanes), F32),
                pltpu.VMEM((fields, rows, lanes), F32),
                pltpu.VMEM((fields, rows, lanes), F32),
                pltpu.VMEM((fields + 1, rows, lanes), F32),
                pltpu.VMEM((fields + 1, rows, lanes), F32),
                pltpu.VMEM((3, rows, lanes), F32),
                pltpu.VMEM((pairs, rows, 2 * lanes), F32),
                pltpu.VMEM((pairs, rows, 2 * lanes), F32),
                pltpu.VMEM((pairs, rows, lanes), F32),
                pltpu.VMEM((pairs, rows, lanes), F32),
                pltpu.VMEM((pairs, rows, lanes), F32),
                pltpu.VMEM((pairs, rows, lanes), F32),
                pltpu.VMEM((members, band, lanes), F32),
                pltpu.VMEM((bands, n_dom, fields + 2, share, lanes), F32),
                pltpu.VMEM((bands, n_dom - 1, fields + 2, share, lanes), F32),
                pltpu.VMEM((bands, fields, share, lanes), F32),
                pltpu.VMEM((bands, n_dom - 1, fields, share, lanes), F32),
                pltpu.VMEM((rows, 3 * rows), BF16),
                pltpu.VMEM((2 * lanes, 2 * lanes), BF16),
                pltpu.VMEM((2 * lanes, 2 * lanes), BF16),
                pltpu.VMEM((3 * lanes, lanes), BF16),
                dma((4,)),
                dma((2, groups)),
                dma((fields + 1, 2)),
                dma((fields + 1, 2)),
                dma((2, pairs + 1)),
                dma((2, pairs + 1)),
                dma((bands, n_dom - 1)),
                dma((bands, n_dom - 1)),
                dma((bands, n_dom - 1)),
                dma((bands, n_dom - 1)),
            ],
            compiler_params=pltpu.CompilerParams(
                collective_id=0, has_side_effects=True, vmem_limit_bytes=62 * 1024 * 1024
            ),
            cost_estimate=pl.CostEstimate(
                flops=200_000_000, bytes_accessed=9_000_000, transcendentals=400_000
            ),
        )(
            ensemble,
            depth_class,
            obs_index.reshape(-1, lanes),
            obs_value.reshape(-1, lanes),
            annealing_exponents,
        )

    in_specs = (P("dom", None, None, "col"), P(None, "col"), P("col"), P("col"), P(None, "col"))
    out_specs = P(None, None, "col")
    return jax.shard_map(
        on_device, mesh=mesh, in_specs=in_specs, out_specs=out_specs, check_vma=False
    )
```

```python
import functools

import jax
import jax.numpy as jnp
from jax import lax
from jax.experimental import pallas as pl
from jax.experimental.pallas import tpu as pltpu
from jax.sharding import PartitionSpec as P

MESH = pl.DeviceIdType.MESH
F32 = jnp.float32
BF16 = jnp.bfloat16

TIME_STEP = 0.25
CORIOLIS = 0.2
HALF_DT = 0.5 * TIME_STEP
DT_F = TIME_STEP * CORIOLIS

ROW_REACH = 8
LANES = 128
PAD = 8
FOLD = 8
SPAN = 16
CHUNK = 32
EARLY = 20
BESIDE = 4
HALF_BAND = 16


def shifted(q, amount):
    return pltpu.roll(q, amount % LANES, q.ndim - 1)


def pieces(q):
    first = q.astype(BF16)
    rest = q - first.astype(F32)
    second = rest.astype(BF16)
    third = (rest - second.astype(F32)).astype(BF16)
    return first, second, third


def lane_of(shape):
    return lax.broadcasted_iota(jnp.int32, shape, len(shape) - 1)


def row_of(shape):
    return lax.broadcasted_iota(jnp.int32, shape, len(shape) - 2)


def dot(a, b):
    return jnp.dot(a, b, preferred_element_type=F32)


def kernel(
    n_dom,
    n_col,
    ens_ref,
    class_ref,
    where_ref,
    value_ref,
    anneal_ref,
    out_ref,
    X,
    U1,
    Y,
    YT,
    DV,
    CLS,
    WHERE,
    VALUE,
    ANNEAL,
    D,
    QD,
    Q,
    FE,
    SL,
    SR,
    RL,
    RR,
    OBS,
    SM,
    PART,
    TOL,
    TOR,
    HL,
    HR,
    LW,
    GIVE,
    TAKE,
    DONE,
    FETCHED,
    RT,
    WOWN,
    WHALO,
    DX,
    small_sem,
    load_sem,
    edge_send,
    edge_recv,
    halo_send,
    halo_recv,
    part_send,
    part_recv,
    out_send,
    out_recv,
):
    members, fields, rows, _ = ens_ref.shape
    groups = members // FOLD
    pairs = members // 2
    share = 8
    band = share * n_dom
    radius = LANES // 2
    flow = 3
    me_dom = lax.axis_index("dom")
    me_col = lax.axis_index("col")
    right = lax.rem(me_col + 1, n_col)
    left = lax.rem(me_col + n_col - 1, n_col)
    inner = pl.ds(PAD, rows)

    def load(g, tracers):
        which = pl.ds(flow, fields - flow) if tracers else pl.ds(0, flow)
        return pltpu.make_async_copy(
            ens_ref.at[pl.ds(g * FOLD, FOLD), which],
            X.at[pl.ds(g * FOLD, FOLD), which, inner, :],
            load_sem.at[int(tracers), g],
        )

    small = [
        pltpu.make_async_copy(source, target, small_sem.at[k])
        for k, (source, target) in enumerate(
            ((class_ref, CLS), (where_ref, WHERE), (value_ref, VALUE), (anneal_ref, ANNEAL))
        )
    ]
    load(0, False).start()
    for copy in small:
        copy.start()
    for g in range(1, groups):
        load(g, False).start()
    for g in range(groups):
        load(g, True).start()

    barrier = pltpu.get_barrier_semaphore()
    for other in (left, right):
        pl.semaphore_signal(barrier, inc=1, device_id=(me_dom, other), device_id_type=MESH)
    for off in range(1, n_dom):
        pl.semaphore_signal(
            barrier,
            inc=1,
            device_id=(lax.rem(me_dom + off, n_dom), me_col),
            device_id_type=MESH,
        )

    zero = jnp.zeros((PAD, LANES), F32)

    def clear(m, carry):
        for f in (0, 3, 4):
            X[m, f, 0:PAD, :] = zero
            X[m, f, PAD + rows : PAD + rows + PAD, :] = zero
        return carry

    lax.fori_loop(0, members + 2 * groups, clear, 0)
    for k in range(BESIDE):
        for padded in (Y.at[k], DV.at[k], YT.at[k, 0], YT.at[k, 1]):
            padded[0:PAD, :] = zero
            padded[PAD + rows : PAD + rows + PAD, :] = zero

    for copy in small:
        copy.wait()

    plane = (rows, LANES)
    lane = lane_of(plane)
    slot = lane % SPAN
    holder = lane // SPAN
    depth = 0.5 + 0.25 * CLS[...].astype(F32)
    D[0] = depth
    packed_depth = shifted(depth, 8)
    for i in range(1, FOLD):
        packed_depth = jnp.where(holder == i, shifted(depth, 8 + SPAN * i), packed_depth)
    QD[...] = packed_depth
    def pack_group(g, first, last):
        for f in range(first, last):
            q = shifted(X[g * FOLD, f, inner, :], 8)
            for i in range(1, FOLD):
                q = jnp.where(
                    holder == i, shifted(X[g * FOLD + i, f, inner, :], 8 + SPAN * i), q
                )
            Q[g, f] = q

    def edges(f):
        keep = (slot >= 4) & (slot < 12)
        even = jnp.where(keep, Q[0, f], shifted(Q[1, f], 8))
        odd = shifted(jnp.where(keep, Q[2, f], shifted(Q[3, f], 8)), 4)
        SR[f] = jnp.where(slot % 8 >= 4, even, odd)
        SL[f] = jnp.where(slot % 8 >= 4, odd, even)

    def send(source, target, there, send_sem, recv_sem):
        return pltpu.make_async_remote_copy(
            src_ref=source,
            dst_ref=target,
            send_sem=send_sem,
            recv_sem=recv_sem,
            device_id=(me_dom, there),
            device_id_type=MESH,
        )

    def edge_copies(f):
        to_left, to_right = (QD, QD) if f == fields else (SL.at[f], SR.at[f])
        return (
            send(to_left, RR.at[f], left, edge_send.at[f, 0], edge_recv.at[f, 0]),
            send(to_right, RL.at[f], right, edge_send.at[f, 1], edge_recv.at[f, 1]),
        )

    travelling = [edge_copies(f) for f in range(fields + 1)]
    moved_by = (0, -8, -4, -12)

    def begin(f):
        for copy in travelling[f]:
            copy.start()

    for g in range(groups):
        load(g, False).wait()
        pack_group(g, 0, 1)
    edges(0)
    pl.semaphore_wait(barrier, 2 + n_dom - 1)
    begin(fields)
    begin(0)
    for f in range(1, fields):
        for g in range(groups):
            if f == flow:
                load(g, True).wait()
            pack_group(g, f, f + 1)
        edges(f)
        begin(f)

    tall = (rows, 3 * rows)
    RT[...] = jnp.maximum(
        0, ROW_REACH + 1 - jnp.abs(row_of(tall) - lane_of(tall) % rows)
    ).astype(F32).astype(BF16)
    wide = (2 * LANES, 2 * LANES)
    to = lane_of(wide)
    have = row_of(wide)
    near = jnp.maximum(0, radius + 1 - jnp.abs(have % LANES - to % LANES))
    WOWN[...] = jnp.where(have // LANES == to // LANES, near, 0).astype(F32).astype(BF16)
    column = have % radius + jnp.where(have < LANES, LANES, -radius)
    near = jnp.maximum(0, radius + 1 - jnp.abs(column - to % LANES))
    WHALO[...] = (
        jnp.where((have % LANES) // radius == to // LANES, near, 0).astype(F32).astype(BF16)
    )

    wide = (3 * LANES, LANES)
    ahead_by = (row_of(wide) - lane_of(wide)) % LANES
    DX[...] = (
        jnp.where(ahead_by == 1, HALF_DT, jnp.where(ahead_by == LANES - 1, -HALF_DT, 0.0))
    ).astype(BF16)

    where = WHERE[...]
    value = VALUE[...]
    parts = where.shape[0]

    def along(q):
        return jnp.concatenate([q[j : j + 1, :] for j in range(parts)], axis=1)

    obs_row = along(where // LANES)
    obs_col = along(where % LANES)
    obs_value = along(value)
    count_obs = parts * LANES
    in_row = row_of((rows, count_obs)) == obs_row
    in_col = row_of((LANES, count_obs)) == obs_col
    cols_hot = jnp.where(in_col, 1.0, 0.0).astype(BF16)

    def on_grid(piece):
        left_side = jnp.where(in_row, piece, 0.0).astype(BF16)
        return lax.dot_general(
            left_side, cols_hot, (((1,), (1,)), ((), ())), preferred_element_type=F32
        )

    def on_grid_exact(values):
        a, b, c = pieces(values)
        return on_grid(a.astype(F32)) + (on_grid(b.astype(F32)) + on_grid(c.astype(F32)))

    count = on_grid(jnp.ones_like(obs_value))
    total_obs = on_grid_exact(obs_value)
    squares = on_grid_exact(obs_value * obs_value)
    mean_obs = total_obs / jnp.maximum(count, 1.0)
    OBS[0] = -0.5 * count
    OBS[1] = mean_obs
    OBS[2] = -0.5 * (squares - total_obs * mean_obs)

    def split_in(q, count):
        found = []
        for k in range(count):
            found.append(q.astype(BF16))
            if k < count - 1:
                q = q - found[-1].astype(F32)
        return jnp.concatenate(found, axis=1)

    def flow_ahead(ms, d):
        for step in range(2):
            ends = [(X.at[m, 0], Y.at[k]) for k, m in enumerate(ms)]
            if step == 1:
                ends = [(target, source) for source, target in ends]
            across = [dot(split_in(h_ref[inner, :], 3), DX[...]) for h_ref, _ in ends]
            steep = []
            for k, m in enumerate(ms):
                h_ref = ends[k][0]
                split = []
                for r in range(0, rows, CHUNK):
                    cut = pl.ds(r, CHUNK)
                    mid = pl.ds(PAD + r, CHUNK)
                    if step == 0:
                        u, v = X[m, 1, mid, :], X[m, 2, mid, :]
                    else:
                        u, v = U1[m, 0, cut, :], U1[m, 1, cut, :]
                    u1 = u - across[k][r : r + CHUNK, :] + DT_F * v
                    slope = (
                        h_ref[pl.ds(PAD + r + 1, CHUNK), :] - h_ref[pl.ds(PAD + r - 1, CHUNK), :]
                    )
                    v1 = v - HALF_DT * slope - DT_F * u
                    if step == 0:
                        U1[m, 0, cut, :] = u1
                        U1[m, 1, cut, :] = v1
                    else:
                        X[m, 1, mid, :] = u1
                        X[m, 2, mid, :] = v1
                    deep = D[d, cut, :]
                    DV[k, mid, :] = deep * v1
                    split.append(split_in(deep * u1, 3))
                steep.append(dot(jnp.concatenate(split, axis=0), DX[...]))
            for k, m in enumerate(ms):
                h_ref, to_ref = ends[k]
                for r in range(0, rows, CHUNK):
                    mid = pl.ds(PAD + r, CHUNK)
                    slope = DV[k, pl.ds(PAD + r + 1, CHUNK), :] - DV[k, pl.ds(PAD + r - 1, CHUNK), :]
                    to_ref[mid, :] = h_ref[mid, :] - (
                        steep[k][r : r + CHUNK, :] + HALF_DT * slope
                    )

    def tracers_ahead(ms):
        for step in range(2):
            steep = []
            for k, m in enumerate(ms):
                for f in range(flow, fields):
                    source = X.at[m, f] if step == 0 else YT.at[k, f - flow]
                    steep.append(split_in(source[inner, :], 2))
            steep = [
                dot(jnp.concatenate(steep[2 * k : 2 * k + 2], axis=0), DX[0 : 2 * LANES, :])
                for k in range(len(ms))
            ]
            for k, m in enumerate(ms):
                ends = [(X.at[m, f], YT.at[k, f - flow]) for f in range(flow, fields)]
                if step == 1:
                    ends = [(target, source) for source, target in ends]
                for r in range(0, rows, CHUNK):
                    mid = pl.ds(PAD + r, CHUNK)
                    if step == 0:
                        u = U1[m, 0, pl.ds(r, CHUNK), :]
                        v = U1[m, 1, pl.ds(r, CHUNK), :]
                    else:
                        u = X[m, 1, mid, :]
                        v = X[m, 2, mid, :]
                    v = HALF_DT * v
                    for j, (source, target) in enumerate(ends):
                        slope = (
                            source[pl.ds(PAD + r + 1, CHUNK), :]
                            - source[pl.ds(PAD + r - 1, CHUNK), :]
                        )
                        across = steep[k][j * rows + r : j * rows + r + CHUNK, :]
                        target[mid, :] = source[mid, :] - (u * across + v * slope)

    def some(first):
        return [first + k for k in range(BESIDE)]

    def flow_main(m, carry):
        flow_ahead(some(BESIDE * m), 0)
        return carry

    early = EARLY
    lax.fori_loop(0, early // BESIDE, flow_main, 0)

    def strips(f, carry):
        for g in range(groups):
            q = Q[g, f]
            X[members + g, f, inner, :] = jnp.where(slot < 8, q, shifted(RR[f], moved_by[g]))
            X[members + groups + g, f, inner, :] = jnp.where(
                slot >= 8, q, shifted(RL[f], moved_by[g])
            )
        return carry

    def join(f, carry):
        for g in range(groups):
            FE[g, f] = jnp.where(
                slot < 8, X[members + g, f, inner, :], X[members + groups + g, f, inner, :]
            )
        return carry

    for f in (fields, 0, 1, 2):
        for copy in travelling[f]:
            copy.wait()
    D[1] = jnp.where(slot < 8, QD[...], RR[fields])
    D[2] = jnp.where(slot >= 8, QD[...], RL[fields])
    lax.fori_loop(0, flow, strips, 0)

    def flow_strip(s, carry):
        flow_ahead(some(members + BESIDE * s), 1 + BESIDE * s // groups)
        return carry

    lax.fori_loop(0, 2 * groups // BESIDE, flow_strip, 0)
    join(0, 0)

    at_edge = (lane < 4) | (lane >= LANES - 4)

    def place(i):
        return lax.rem(LANES + LANES - 8 - SPAN * i, LANES)

    upper = rows - band

    def halo_pair(p):
        here = pl.ds(0, upper)
        return (
            send(TOL.at[p, here], HR.at[p, here], left, halo_send.at[0, p], halo_recv.at[0, p]),
            send(TOR.at[p, here], HL.at[p, here], right, halo_send.at[1, p], halo_recv.at[1, p]),
        )

    def halo_rest():
        here = pl.ds(upper, band)
        return (
            send(
                TOL.at[:, here], HR.at[:, here], left, halo_send.at[0, pairs], halo_recv.at[0, pairs]
            ),
            send(
                TOR.at[:, here], HL.at[:, here], right, halo_send.at[1, pairs], halo_recv.at[1, pairs]
            ),
        )

    def likelihood(ps):
        logs = []
        for p in ps:
            both = []
            for k in range(2):
                m = 2 * p + k
                edge = pltpu.roll(FE[m // FOLD, 0], place(lax.rem(m, FOLD)), 1)
                h = jnp.where(at_edge, edge, X[m, 0, inner, :])
                miss = OBS[1] - h
                both.append(OBS[0] * (miss * miss) + OBS[2])
            logs.append(jnp.concatenate(both, axis=1))
        smoothed = [dot(RT[...], jnp.concatenate(pieces(q), axis=0)) for q in logs]
        for p, smooth in zip(ps, smoothed):
            SM[p] = smooth
            first, second = smooth[:, :LANES], smooth[:, LANES:]
            low = lane < radius
            turned = shifted(jnp.where(low, second, first), radius)
            TOL[p] = jnp.where(low, first, turned)
            TOR[p] = jnp.where(low, turned, second)
            for copy in halo_pair(p):
                copy.start()

    def flow_and_likelihood(q, carry):
        flow_ahead(some(BESIDE * q + early), 0)
        likelihood([2 * q + 2, 2 * q + 3])
        return carry

    def only_likelihood(q, carry):
        likelihood([2 * q, 2 * q + 1])
        return carry

    both_ways = (members - early) // BESIDE
    likelihood([0, 1])
    lax.fori_loop(0, both_ways, flow_and_likelihood, 0)
    lax.fori_loop(both_ways + 1, pairs // 2, only_likelihood, 0)
    for copy in halo_rest():
        copy.start()

    def tracers_main(m, carry):
        tracers_ahead(some(BESIDE * m))
        return carry

    for f in range(flow, fields):
        for copy in travelling[f]:
            copy.wait()
    lax.fori_loop(flow, fields, strips, 0)
    lax.fori_loop(0, (members + 2 * groups) // BESIDE, tracers_main, 0)
    lax.fori_loop(1, fields, join, 0)

    def columns(q, table):
        a, b, c = pieces(q)
        return dot(a, table) + (dot(b, table) + dot(c, table))

    def own_columns(p, carry):
        PART[p] = columns(SM[p], WOWN[...])
        return carry

    lax.fori_loop(0, pairs, own_columns, 0, unroll=8)

    def halo_wait(p, carry):
        for copy in halo_pair(p):
            copy.wait()
        return carry

    scale = 1.0 / ((ROW_REACH + 1.0) * (radius + 1.0))
    cut = (HALF_BAND, LANES)
    cut_lane = lane_of(cut)
    cut_edge = (cut_lane < 4) | (cut_lane >= LANES - 4)
    cut_holder = cut_lane // SPAN

    def weigh(b):
        here = pl.ds(b * band, band)
        halo = jnp.concatenate([HR[:, here, :], HL[:, here, :]], axis=2)
        smooth = PART[:, here, :].reshape(pairs * band, 2 * LANES) + columns(
            halo.reshape(pairs * band, 2 * LANES), WHALO[...]
        )
        smooth = smooth.reshape(pairs, band, 2 * LANES)
        power = ANNEAL[here, :] * scale
        peak = None
        for p in range(pairs):
            for k in range(2):
                logw = power * smooth[p, :, k * LANES : (k + 1) * LANES]
                LW[2 * p + k] = logw
                peak = logw if peak is None else jnp.maximum(peak, logw)
        def set_out(f, start, q):
            for d in range(start // share, (start + q.shape[0]) // share):
                GIVE[b, d, f] = q[d * share - start : (d + 1) * share - start, :]

        set_out(0, 0, peak)
        for start in range(0, band, HALF_BAND):
            within = pl.ds(start, HALF_BAND)
            here = pl.ds(b * band + start, HALF_BAND)
            there = pl.ds(PAD + b * band + start, HALF_BAND)
            best = peak[start : start + HALF_BAND, :]
            total = jnp.zeros(cut, F32)
            sums = [jnp.zeros(cut, F32) for _ in range(fields)]
            edge_sums = [jnp.zeros(cut, F32) for _ in range(fields)]
            for g in range(groups):
                packed = None
                for i in range(FOLD):
                    m = g * FOLD + i
                    w = jnp.exp(LW[m, within, :] - best)
                    total = total + w
                    for f in range(fields):
                        sums[f] = sums[f] + w * X[m, f, there, :]
                    moved = shifted(w, 8 + SPAN * i)
                    packed = moved if packed is None else jnp.where(cut_holder == i, moved, packed)
                for f in range(fields):
                    edge_sums[f] = edge_sums[f] + packed * FE[g, f, here, :]
            set_out(1, start, total)
            for f in range(fields):
                e = edge_sums[f]
                e = e + shifted(e, SPAN)
                e = e + shifted(e, 2 * SPAN)
                e = e + shifted(e, 4 * SPAN)
                set_out(2 + f, start, jnp.where(cut_edge, shifted(e, LANES - 8), sums[f]))

    def give(b, off):
        owner = lax.rem(me_dom + off, n_dom)
        return pltpu.make_async_remote_copy(
            src_ref=GIVE.at[b, owner],
            dst_ref=TAKE.at[b, off - 1],
            send_sem=part_send.at[b, off - 1],
            recv_sem=part_recv.at[b, off - 1],
            device_id=(owner, me_col),
            device_id_type=MESH,
        )

    def hand_out(b, off):
        return pltpu.make_async_remote_copy(
            src_ref=DONE.at[b],
            dst_ref=FETCHED.at[b, off - 1],
            send_sem=out_send.at[b, off - 1],
            recv_sem=out_recv.at[b, off - 1],
            device_id=(lax.rem(me_dom + off, n_dom), me_col),
            device_id_type=MESH,
        )

    far_first = (2, 1, 3)

    def join_band(b):
        for off in far_first:
            give(b, off).wait()
        peaks = [GIVE[b, me_dom, 0]] + [TAKE[b, k, 0] for k in range(n_dom - 1)]
        peak = functools.reduce(jnp.maximum, peaks)
        factors = [jnp.exp(q - peak) for q in peaks]

        def joined(f):
            result = factors[0] * GIVE[b, me_dom, f]
            for k in range(n_dom - 1):
                result = result + factors[k + 1] * TAKE[b, k, f]
            return result

        total = joined(1)
        for f in range(fields):
            DONE[b, f] = joined(2 + f) / total
        for off in far_first:
            hand_out(b, off).start()

    bands = rows // band
    lax.fori_loop(0, pairs, halo_wait, 0)
    for b in range(bands):
        if b == bands - 1:
            for copy in halo_rest():
                copy.wait()
        weigh(b)
        for off in far_first:
            give(b, off).start()
    for b in range(bands):
        join_band(b)
    def place_rows(b, d, source):
        here = pl.ds(pl.multiple_of(b * band + d * share, 8), share)
        for f in range(fields):
            out_ref[f, here, :] = source[f]

    for b in range(bands):
        place_rows(b, me_dom, DONE.at[b])
        for off in far_first:
            hand_out(b, off).wait()
            place_rows(b, lax.rem(me_dom + n_dom - off, n_dom), FETCHED.at[b, off - 1])


def solution(mesh):
    n_dom = mesh.shape["dom"]
    n_col = mesh.shape["col"]

    def on_device(ensemble, depth_class, obs_index, obs_value, annealing_exponents):
        members, fields, rows, lanes = ensemble.shape
        groups = members // FOLD
        pairs = members // 2
        share = 8
        band = share * n_dom
        bands = rows // band
        tall = rows + 2 * PAD
        vm = pl.BlockSpec(memory_space=pltpu.VMEM)
        dma = pltpu.SemaphoreType.DMA
        return pl.pallas_call(
            functools.partial(kernel, n_dom, n_col),
            out_shape=jax.ShapeDtypeStruct((fields, rows, lanes), F32),
            in_specs=[pl.BlockSpec(memory_space=pl.ANY)] * 5,
            out_specs=vm,
            scratch_shapes=[
                pltpu.VMEM((members + 2 * groups, fields, tall, lanes), F32),
                pltpu.VMEM((members + 2 * groups, 2, rows, lanes), F32),
                pltpu.VMEM((BESIDE, tall, lanes), F32),
                pltpu.VMEM((BESIDE, 2, tall, lanes), F32),
                pltpu.VMEM((BESIDE, tall, lanes), F32),
                pltpu.VMEM((rows, lanes), jnp.int32),
                pltpu.VMEM((obs_index.shape[0] // lanes, lanes), jnp.int32),
                pltpu.VMEM((obs_index.shape[0] // lanes, lanes), F32),
                pltpu.VMEM((rows, lanes), F32),
                pltpu.VMEM((3, rows, lanes), F32),
                pltpu.VMEM((rows, lanes), F32),
                pltpu.VMEM((groups, fields, rows, lanes), F32),
                pltpu.VMEM((groups, fields, rows, lanes), F32),
                pltpu.VMEM((fields, rows, lanes), F32),
                pltpu.VMEM((fields, rows, lanes), F32),
                pltpu.VMEM((fields + 1, rows, lanes), F32),
                pltpu.VMEM((fields + 1, rows, lanes), F32),
                pltpu.VMEM((3, rows, lanes), F32),
                pltpu.VMEM((pairs, rows, 2 * lanes), F32),
                pltpu.VMEM((pairs, rows, 2 * lanes), F32),
                pltpu.VMEM((pairs, rows, lanes), F32),
                pltpu.VMEM((pairs, rows, lanes), F32),
                pltpu.VMEM((pairs, rows, lanes), F32),
                pltpu.VMEM((pairs, rows, lanes), F32),
                pltpu.VMEM((members, band, lanes), F32),
                pltpu.VMEM((bands, n_dom, fields + 2, share, lanes), F32),
                pltpu.VMEM((bands, n_dom - 1, fields + 2, share, lanes), F32),
                pltpu.VMEM((bands, fields, share, lanes), F32),
                pltpu.VMEM((bands, n_dom - 1, fields, share, lanes), F32),
                pltpu.VMEM((rows, 3 * rows), BF16),
                pltpu.VMEM((2 * lanes, 2 * lanes), BF16),
                pltpu.VMEM((2 * lanes, 2 * lanes), BF16),
                pltpu.VMEM((3 * lanes, lanes), BF16),
                dma((4,)),
                dma((2, groups)),
                dma((fields + 1, 2)),
                dma((fields + 1, 2)),
                dma((2, pairs + 1)),
                dma((2, pairs + 1)),
                dma((bands, n_dom - 1)),
                dma((bands, n_dom - 1)),
                dma((bands, n_dom - 1)),
                dma((bands, n_dom - 1)),
            ],
            compiler_params=pltpu.CompilerParams(
                collective_id=0, has_side_effects=True, vmem_limit_bytes=62 * 1024 * 1024
            ),
            cost_estimate=pl.CostEstimate(
                flops=200_000_000, bytes_accessed=9_000_000, transcendentals=400_000
            ),
        )(
            ensemble,
            depth_class,
            obs_index.reshape(-1, lanes),
            obs_value.reshape(-1, lanes),
            annealing_exponents,
        )

    in_specs = (P("dom", None, None, "col"), P(None, "col"), P("col"), P("col"), P(None, "col"))
    out_specs = P(None, None, "col")
    return jax.shard_map(
        on_device, mesh=mesh, in_specs=in_specs, out_specs=out_specs, check_vma=False
    )
```
